32 devices in a mesh: lsec: 4 (over x, core), rsec: 4 (over z), ops: 2 (over y).
Axes of the slice: x: 2, y: 2, z: 4, core: 2. Of those that a mesh axis runs over, the one named last changes fastest.
Arguments:
- psi: bfloat16 [16, 16, 128, 128], P(('lsec', 'rsec')), may hold values from -6 to 6
- left_ops: bfloat16 [4, 16, 128, 128], P('ops', ('lsec', 'rsec')), may hold values from -0.5 to 0.5
- right_ops: bfloat16 [4, 16, 128, 128], P('ops', ('lsec', 'rsec')), may hold values from -0.25 to 0.25
- left_order: int32 [16], replicated, may hold values from 0 to 15, each once
- right_order: int32 [16], replicated, may hold values from 0 to 15, each once
- left_qn: int32 [16], replicated, may hold values from 0 to 2
- right_qn: int32 [16], replicated, may hold values from 0 to 2
- left_dims: int32 [16], replicated, may hold values from 96 to 128
- right_dims: int32 [16], replicated, may hold values from 96 to 128
Outputs:
- first_sigma: bfloat16 [16, 16, 128, 128], P(('lsec', 'rsec'))
- second_sigma: bfloat16 [16, 16, 128, 128], P(('lsec', 'rsec'), 'ops')
The draws below stay inside these ranges and needn't reach their ends.
Inputs may be any that keep to these rules, and one draw needn't show every extreme that they name: left_order holds each left sector once. right_order holds each right sector once.
All inputs are finite; a program needn't handle non-finite values.
Results may differ from the reference program's by a relative error of at most 0.025.
Values may be sent and summed in bfloat16 or wider, within the bound.
A program may use at most 64 MiB of HBM per device.

```python
import jax
import jax.numpy as jnp
from jax import lax

M = 128
K_DEV = 2
QMAX = 3
SPREAD = 1
K = 4
NL = 16
NR = 16
N_OPS = 2


def place_ends(result, key, low, largest):
    extent = result.shape
    place = [jax.random.randint(jax.random.fold_in(key, axis), (), 0, extent[axis]) for axis in range(len(extent))]
    result = result.at[tuple(place)].set(low)
    longest = extent.index(max(extent))
    place[longest] = (place[longest] + 1) % extent[longest]
    return result.at[tuple(place)].set(largest)


def levels(stream_key, extent, shards, least, top_value):
    factor_of = 1.0
    for dim, parts in shards:
        heights = jax.random.uniform(jax.random.fold_in(jax.random.fold_in(stream_key, 6), dim), (parts,), jnp.float32, least / len(shards), top_value / len(shards))
        factor_of = factor_of * jnp.repeat(jnp.exp(heights), extent[dim] // parts).reshape((-1,) + (1,) * (len(extent) - 1 - dim))
    return factor_of


def normal_values(rng, dims, spread, bound, pieces=(), kind=jnp.bfloat16):
    entries = spread * jax.random.normal(rng, dims, jnp.float32)
    if pieces:
        entries = entries * levels(rng, dims, pieces, -0.22, 0.18)
    return jnp.clip(entries, -bound, bound).astype(kind)


def setup_inputs(seed: int = 0) -> dict:
    key_of = jax.random.split(jax.random.key(seed), 10)
    psi = normal_values(key_of[0], (NL, NR, M, M), 1.0, 6.0, ((0, 16),))
    left_ops = normal_values(key_of[1], (K, NL, M, M), M ** -0.5, 0.5, ((0, 2), (1, 16)))
    right_ops = normal_values(key_of[2], (K, NR, M, M), (M * K) ** -0.5, 0.25, ((0, 2), (1, 16)))
    left_order = jax.random.permutation(key_of[3], NL).astype(jnp.int32)
    right_order = jax.random.permutation(key_of[4], NR).astype(jnp.int32)
    left_qn = place_ends(jax.random.randint(key_of[5], (NL,), 0, QMAX), jax.random.fold_in(key_of[5], 1), 0, QMAX - 1).astype(jnp.int32)
    right_qn = place_ends(jax.random.randint(key_of[6], (NR,), 0, QMAX), jax.random.fold_in(key_of[6], 1), 0, QMAX - 1).astype(jnp.int32)
    left_dims = place_ends(jax.random.randint(key_of[7], (NL,), 3 * M // 4, M + 1), jax.random.fold_in(key_of[7], 1), 3 * M // 4, M).astype(jnp.int32)
    right_dims = place_ends(jax.random.randint(key_of[8], (NR,), 3 * M // 4, M + 1), jax.random.fold_in(key_of[8], 1), 3 * M // 4, M).astype(jnp.int32)
    return {"psi": psi, "left_ops": left_ops, "right_ops": right_ops, "left_order": left_order, "right_order": right_order, "left_qn": left_qn, "right_qn": right_qn, "left_dims": left_dims, "right_dims": right_dims}


def projector(left_qn, right_qn, left_dims, right_dims):
    allowed = jnp.abs(left_qn[:, None] - right_qn[None, :]) <= SPREAD
    line = jnp.arange(M, dtype=jnp.int32)
    rows = line[None, :] < left_dims[:, None]
    cols = line[None, :] < right_dims[:, None]
    return allowed[:, :, None, None] & rows[:, None, :, None] & cols[None, :, None, :]


def inverse(order, count):
    return jnp.zeros((count,), jnp.int32).at[order].set(jnp.arange(count, dtype=jnp.int32))


def apply_terms(state, left_id, right_id, left_first):
    values = state.astype(jnp.float32)

    def group(total, group_index):
        def term(acc, inner_index):
            k = group_index * K_DEV + inner_index
            left_block = left_id[k].astype(jnp.float32)
            right_block = right_id[k].astype(jnp.float32)
            if left_first:
                inner = jnp.einsum("axy,abyz->abxz", left_block, values).astype(jnp.bfloat16)
                inner = lax.optimization_barrier(inner).astype(jnp.float32)
                outer = jnp.einsum("abxy,bzy->abxz", inner, right_block)
            else:
                inner = jnp.einsum("abxy,bzy->abxz", values, right_block).astype(jnp.bfloat16)
                inner = lax.optimization_barrier(inner).astype(jnp.float32)
                outer = jnp.einsum("axy,abyz->abxz", left_block, inner)
            return acc + outer, None

        part, _ = lax.scan(term, jnp.zeros(values.shape, jnp.float32), jnp.arange(K_DEV, dtype=jnp.int32))
        part = lax.optimization_barrier(part.astype(jnp.bfloat16)).astype(jnp.float32)
        return total + part, None

    summed, _ = lax.scan(group, jnp.zeros(values.shape, jnp.float32), jnp.arange(N_OPS, dtype=jnp.int32))
    return summed


def reference(psi, left_ops, right_ops, left_order, right_order, left_qn, right_qn, left_dims, right_dims):
    inv_left = inverse(left_order, NL)
    inv_right = inverse(right_order, NR)
    mask = projector(left_qn, right_qn, left_dims, right_dims)
    left_id = left_ops[:, inv_left]
    right_id = right_ops[:, inv_right]
    start = jnp.where(mask, psi[inv_left], jnp.zeros((), jnp.bfloat16))
    first_id = jnp.where(mask, apply_terms(start, left_id, right_id, True), 0.0).astype(jnp.bfloat16)
    second_id = jnp.where(mask, apply_terms(first_id, left_id, right_id, False), 0.0).astype(jnp.bfloat16)
    first_sigma = jnp.transpose(first_id[:, right_order], (1, 0, 2, 3))
    second_sigma = second_id[left_order]
    return first_sigma, second_sigma
```

```python
import functools

import jax
import jax.numpy as jnp
from jax import lax
from jax.experimental import pallas as pl
from jax.experimental.pallas import tpu as pltpu
from jax.sharding import PartitionSpec as P

SPREAD = 1
VMEM_BUDGET = 24 * 2**20
MESH = pl.DeviceIdType.MESH
NT = (((1,), (1,)), ((), ()))


def relayout(blocks):
    return lax.all_to_all(blocks, ("lsec", "rsec"), split_axis=1, concat_axis=1, tiled=True)


def inverse(order):
    count = order.shape[0]
    return jnp.zeros((count,), jnp.int32).at[order].set(jnp.arange(count, dtype=jnp.int32))


def by_collectives(
    psi, left_ops, right_ops, left_order, right_order, left_qn, right_qn, left_dims, right_dims
):
    slot = lax.axis_index(("lsec", "rsec"))
    width = psi.shape[-1]
    line = jnp.arange(width, dtype=jnp.int32)
    left_sector = left_order[slot]
    right_sector = right_order[slot]
    inv_left = inverse(left_order)
    inv_right = inverse(right_order)
    left_here = left_ops[:, 0]
    right_here = right_ops[:, 0]
    allowed_row = jnp.abs(left_qn[left_sector] - right_qn) <= SPREAD
    row_used = line < left_dims[left_sector]
    col_used = line[None, :] < right_dims[:, None]
    mask_left = allowed_row[:, None, None] & row_used[None, :, None] & col_used[:, None, :]
    allowed_col = jnp.abs(left_qn - right_qn[right_sector]) <= SPREAD
    rows_used = line[None, :] < left_dims[:, None]
    cols_here = line < right_dims[right_sector]
    mask_right = allowed_col[:, None, None] & rows_used[:, :, None] & cols_here[None, None, :]
    start = jnp.where(mask_left, psi[0], jnp.zeros((), jnp.bfloat16))
    start_slots = start[right_order]
    lefted = jnp.einsum(
        "kxy,byz->kbxz", left_here, start_slots, preferred_element_type=jnp.float32
    ).astype(jnp.bfloat16)
    arrived = relayout(lefted)
    partial_value = jnp.einsum(
        "kixy,kzy->ixz", arrived, right_here, preferred_element_type=jnp.float32
    )
    partial_value = partial_value[inv_left]
    summed = lax.psum(partial_value.astype(jnp.bfloat16), "ops").astype(jnp.float32)
    first = jnp.where(mask_right, summed, 0.0).astype(jnp.bfloat16)
    first_slots = first[left_order]
    righted = jnp.einsum(
        "ixy,kzy->kixz", first_slots, right_here, preferred_element_type=jnp.float32
    ).astype(jnp.bfloat16)
    returned = relayout(righted)
    second_partial = jnp.einsum(
        "kxy,kjyz->jxz", left_here, returned, preferred_element_type=jnp.float32
    )
    second_partial = second_partial[inv_right]
    second_share = lax.psum_scatter(
        second_partial.astype(jnp.bfloat16), "ops", scatter_dimension=0, tiled=True
    ).astype(jnp.float32)
    count = second_share.shape[0]
    mask_second = lax.dynamic_slice_in_dim(mask_left, lax.axis_index("ops") * count, count, 0)
    second = jnp.where(mask_second, second_share, 0.0).astype(jnp.bfloat16)
    return (first[None], second[None])


def kernel(
    nz,
    nl,
    psi_ref,
    left_ref,
    right_ref,
    left_order,
    right_order,
    left_qn,
    right_qn,
    left_dims,
    right_dims,
    first_ref,
    second_ref,
    rbuf,
    lbuf,
    start,
    terms,
    sigma,
    landed,
    lsend,
    lrecv,
    zsend,
    zrecv,
    xsend,
    xrecv,
    ysend,
    yrecv,
    dsend,
    drecv,
    csend,
    crecv,
    ssend,
    srecv,
):
    l = lax.axis_index("lsec")
    z = lax.axis_index("rsec")
    o = lax.axis_index("ops")
    xp = (l + 2) % nl
    cp = l + 1 - 2 * (l % 2)
    op = 1 - o
    me = l * nz + z
    slots = nl * nz
    width = psi_ref.shape[-1]
    kdev = left_ref.shape[0]
    to_y = {"ops": op}
    to_x = {"lsec": xp}
    to_c = {"lsec": cp}
    sent = []

    def send(src, dst, send_sem, recv_sem, where):
        copy = pltpu.make_async_remote_copy(
            src_ref=src,
            dst_ref=dst,
            send_sem=send_sem,
            recv_sem=recv_sem,
            device_id=where,
            device_id_type=MESH,
        )
        copy.start()
        sent.append(copy)

    def arrive(ref, sem):
        pltpu.make_async_copy(ref, ref, sem).wait()

    rbuf[o, me] = right_ref[:, 0]
    lbuf[o] = left_ref[:, 0]

    barrier = pltpu.get_barrier_semaphore()
    for s in range(nz):
        for t in range(nl):
            if s or t:
                pl.semaphore_signal(
                    barrier,
                    inc=1,
                    device_id={"lsec": (l + t) % nl, "rsec": (z + s) % nz},
                    device_id_type=MESH,
                )
    pl.semaphore_signal(barrier, inc=1, device_id=to_y, device_id_type=MESH)
    pl.semaphore_wait(barrier, slots)

    def slot_of(lane, s):
        return lane * nz + (z + s) % nz

    send(lbuf.at[o], lbuf.at[o], lsend, lrecv, to_y)

    def stage_one(s):
        if s:
            arrive(rbuf.at[o, slot_of(l, s)], zrecv.at[s])
        piece = rbuf.at[o, slot_of(l, s)]
        send(piece, piece, ysend.at[s], yrecv.at[s], to_y)
        send(piece, piece, xsend.at[s], xrecv.at[s], to_x)
        send(piece, piece, csend.at[0, s], crecv.at[0, s], to_c)

    def stage_two(s):
        from_x = rbuf.at[o, slot_of(xp, s)]
        arrive(from_x, xrecv.at[s])
        half = rbuf.at[o, slot_of(xp, s), 0]
        send(half, half, dsend.at[0, s], drecv.at[0, s], to_y)
        send(from_x, from_x, csend.at[1, s], crecv.at[1, s], to_c)
        from_y = rbuf.at[op, slot_of(l, s)]
        arrive(from_y, yrecv.at[s])
        rest = rbuf.at[op, slot_of(l, s), pl.ds(1, kdev - 1)]
        send(rest, rest, dsend.at[1, s], drecv.at[1, s], to_x)
        send(from_y, from_y, csend.at[2, s], crecv.at[2, s], to_c)

    def stage_three(s):
        piece = rbuf.at[op, slot_of(xp, s)]
        arrive(rbuf.at[op, slot_of(xp, s), 0], drecv.at[0, s])
        arrive(rbuf.at[op, slot_of(xp, s), pl.ds(1, kdev - 1)], drecv.at[1, s])
        send(piece, piece, csend.at[3, s], crecv.at[3, s], to_c)

    def stage_four(s):
        cx = (cp + 2) % nl
        arrive(rbuf.at[o, slot_of(cp, s)], crecv.at[0, s])
        arrive(rbuf.at[o, slot_of(cx, s)], crecv.at[1, s])
        arrive(rbuf.at[op, slot_of(cp, s)], crecv.at[2, s])
        arrive(rbuf.at[op, slot_of(cx, s)], crecv.at[3, s])

    for s in range(1, nz):
        piece = rbuf.at[o, me]
        send(piece, piece, zsend.at[s], zrecv.at[s], {"rsec": (z + nz - s) % nz})
    stage_one(0)

    sector = left_order[me]
    my_qn = left_qn[sector]
    rows = lax.broadcasted_iota(jnp.int32, (width, width), 0)
    cols = lax.broadcasted_iota(jnp.int32, (width, width), 1)
    rows_used = rows < left_dims[sector]

    def masked(value, b):
        used = jnp.where(jnp.abs(my_qn - right_qn[b]) <= SPREAD, right_dims[b], 0)
        return jnp.where(rows_used & (cols < used), value, 0.0).astype(jnp.bfloat16)

    def left_terms(half, pair):
        both = jnp.dot(
            lbuf[half].reshape(kdev * width, width), start[pair], preferred_element_type=jnp.float32
        ).astype(jnp.bfloat16)
        both = both.reshape(kdev, width, 2 * width)
        terms[2 * pair, half] = both[:, :, :width]
        terms[2 * pair + 1, half] = both[:, :, width:]

    def own_terms(pair, carry):
        blocks = []
        for j in (2 * pair, 2 * pair + 1):
            b = right_order[j]
            blocks.append(masked(psi_ref[0, b].astype(jnp.float32), b))
        start[pair] = jnp.concatenate(blocks, axis=1)
        left_terms(o, pair)
        return carry

    def other_terms(pair, carry):
        left_terms(op, pair)
        return carry

    lax.fori_loop(0, slots // 2, own_terms, 0)
    stage_one(1)
    stage_two(0)
    arrive(lbuf.at[op], lrecv)
    lax.fori_loop(0, slots // 2, other_terms, 0)

    def lanes(ref, j):
        return jnp.concatenate([ref[j, h, k] for h in range(2) for k in range(kdev)], axis=1)

    def right_lanes(j):
        return jnp.concatenate([rbuf[h, j, k] for h in range(2) for k in range(kdev)], axis=1)

    def first_blocks(s):
        for t in range(nl):
            j = slot_of((l + t) % nl, s)
            value = lax.dot_general(
                lanes(terms, j), right_lanes(j), NT, preferred_element_type=jnp.float32
            )
            sigma[j] = masked(value, right_order[j])
        for t in range(nl):
            j = slot_of((l + t) % nl, s)
            if s or t:
                send(
                    sigma.at[j],
                    landed.at[me],
                    ssend.at[s, t],
                    srecv.at[s, t],
                    {"lsec": (l + t) % nl, "rsec": (z + s) % nz},
                )
            else:
                landed[me] = sigma[j]

    for step in range(2, nz + 3):
        if step < nz:
            stage_one(step)
        if 1 <= step - 1 < nz:
            stage_two(step - 1)
        if 0 <= step - 2 < nz:
            stage_three(step - 2)
        if 0 <= step - 3 < nz:
            stage_four(step - 3)
            first_blocks(step - 3)

    def slot_holding(order, wanted):
        found = jnp.int32(0)
        for j in range(slots):
            found = jnp.where(order[j] == wanted, j, found)
        return found

    count = second_ref.shape[1]

    def second_block(i, carry):
        b = o * count + i
        j = slot_holding(right_order, b)
        state = sigma[j]
        value = None
        for h in range(2):
            for k in range(kdev):
                inner = lax.dot_general(
                    state, rbuf[h, j, k], NT, preferred_element_type=jnp.float32
                ).astype(jnp.bfloat16)
                outer = jnp.dot(lbuf[h, k], inner, preferred_element_type=jnp.float32)
                value = outer if value is None else value + outer
        second_ref[0, i] = masked(value, b)
        return carry

    lax.fori_loop(0, count, second_block, 0, unroll=2)

    for s in range(nz):
        for t in range(nl):
            if s or t:
                source = ((l + nl - t) % nl) * nz + (z + nz - s) % nz
                arrive(landed.at[source], srecv.at[s, t])

    def place(a, carry):
        first_ref[0, a] = landed[slot_holding(left_order, a)]
        return carry

    lax.fori_loop(0, slots, place, 0)

    for copy in sent:
        copy.wait_send()


def by_kernel(nz, nl, psi, left_ops, right_ops, *tables):
    slots = nl * nz
    width = psi.shape[-1]
    kdev = left_ops.shape[0]
    block = (width, width)
    dma = pltpu.SemaphoreType.DMA
    bf16 = jnp.bfloat16
    vmem = pl.BlockSpec(memory_space=pltpu.VMEM)
    smem = pl.BlockSpec(memory_space=pltpu.SMEM)
    flops = 2 * width**3 * 2 * kdev * slots * 3
    return pl.pallas_call(
        functools.partial(kernel, nz, nl),
        out_shape=(
            jax.ShapeDtypeStruct((1, slots) + block, bf16),
            jax.ShapeDtypeStruct((1, slots // 2) + block, bf16),
        ),
        in_specs=[vmem] * 3 + [smem] * 6,
        out_specs=(vmem, vmem),
        scratch_shapes=[
            pltpu.VMEM((2, slots, kdev) + block, bf16),
            pltpu.VMEM((2, kdev) + block, bf16),
            pltpu.VMEM((slots // 2, width, 2 * width), bf16),
            pltpu.VMEM((slots, 2, kdev) + block, bf16),
            pltpu.VMEM((slots,) + block, bf16),
            pltpu.VMEM((slots,) + block, bf16),
            dma,
            dma,
            dma((nz,)),
            dma((nz,)),
            dma((nz,)),
            dma((nz,)),
            dma((nz,)),
            dma((nz,)),
            dma((2, nz)),
            dma((2, nz)),
            dma((4, nz)),
            dma((4, nz)),
            dma((nz, nl)),
            dma((nz, nl)),
        ],
        compiler_params=pltpu.CompilerParams(
            collective_id=0, has_side_effects=True, vmem_limit_bytes=40 * 2**20
        ),
        cost_estimate=pl.CostEstimate(flops=flops, bytes_accessed=4 * 2**20, transcendentals=0),
    )(psi, left_ops, right_ops, *tables)


def solution(mesh):
    nl, nz, no = mesh.shape["lsec"], mesh.shape["rsec"], mesh.shape["ops"]

    def on_device(psi, left_ops, right_ops, *tables):
        gathered = no * nl * nz * left_ops.size * left_ops.dtype.itemsize
        if no == 2 and nl == 4 and left_ops.shape[0] > 1 and 3 * gathered <= VMEM_BUDGET:
            return by_kernel(nz, nl, psi, left_ops, right_ops, *tables)
        return by_collectives(psi, left_ops, right_ops, *tables)

    placed = (
        P(("lsec", "rsec"), None, None, None),
        P("ops", ("lsec", "rsec"), None, None),
        P("ops", ("lsec", "rsec"), None, None),
        P(),
        P(),
        P(),
        P(),
        P(),
        P(),
    )
    return jax.shard_map(
        on_device,
        mesh=mesh,
        in_specs=placed,
        out_specs=(P(("lsec", "rsec"), None, None, None), P(("lsec", "rsec"), "ops", None, None)),
        check_vma=False,
    )
```

```python
import functools

import jax
import jax.numpy as jnp
from jax import lax
from jax.experimental import pallas as pl
from jax.experimental.pallas import tpu as pltpu
from jax.sharding import PartitionSpec as P

SPREAD = 1
VMEM_BUDGET = 24 * 2**20
MESH = pl.DeviceIdType.MESH
NT = (((1,), (1,)), ((), ()))


def relayout(blocks):
    return lax.all_to_all(blocks, ("lsec", "rsec"), split_axis=1, concat_axis=1, tiled=True)


def inverse(order):
    count = order.shape[0]
    return jnp.zeros((count,), jnp.int32).at[order].set(jnp.arange(count, dtype=jnp.int32))


def by_collectives(
    psi, left_ops, right_ops, left_order, right_order, left_qn, right_qn, left_dims, right_dims
):
    slot = lax.axis_index(("lsec", "rsec"))
    width = psi.shape[-1]
    line = jnp.arange(width, dtype=jnp.int32)
    left_sector = left_order[slot]
    right_sector = right_order[slot]
    inv_left = inverse(left_order)
    inv_right = inverse(right_order)
    left_here = left_ops[:, 0]
    right_here = right_ops[:, 0]
    allowed_row = jnp.abs(left_qn[left_sector] - right_qn) <= SPREAD
    row_used = line < left_dims[left_sector]
    col_used = line[None, :] < right_dims[:, None]
    mask_left = allowed_row[:, None, None] & row_used[None, :, None] & col_used[:, None, :]
    allowed_col = jnp.abs(left_qn - right_qn[right_sector]) <= SPREAD
    rows_used = line[None, :] < left_dims[:, None]
    cols_here = line < right_dims[right_sector]
    mask_right = allowed_col[:, None, None] & rows_used[:, :, None] & cols_here[None, None, :]
    start = jnp.where(mask_left, psi[0], jnp.zeros((), jnp.bfloat16))
    start_slots = start[right_order]
    lefted = jnp.einsum(
        "kxy,byz->kbxz", left_here, start_slots, preferred_element_type=jnp.float32
    ).astype(jnp.bfloat16)
    arrived = relayout(lefted)
    partial_value = jnp.einsum(
        "kixy,kzy->ixz", arrived, right_here, preferred_element_type=jnp.float32
    )
    partial_value = partial_value[inv_left]
    summed = lax.psum(partial_value.astype(jnp.bfloat16), "ops").astype(jnp.float32)
    first = jnp.where(mask_right, summed, 0.0).astype(jnp.bfloat16)
    first_slots = first[left_order]
    righted = jnp.einsum(
        "ixy,kzy->kixz", first_slots, right_here, preferred_element_type=jnp.float32
    ).astype(jnp.bfloat16)
    returned = relayout(righted)
    second_partial = jnp.einsum(
        "kxy,kjyz->jxz", left_here, returned, preferred_element_type=jnp.float32
    )
    second_partial = second_partial[inv_right]
    second_share = lax.psum_scatter(
        second_partial.astype(jnp.bfloat16), "ops", scatter_dimension=0, tiled=True
    ).astype(jnp.float32)
    count = second_share.shape[0]
    mask_second = lax.dynamic_slice_in_dim(mask_left, lax.axis_index("ops") * count, count, 0)
    second = jnp.where(mask_second, second_share, 0.0).astype(jnp.bfloat16)
    return (first[None], second[None])


def kernel(
    nz,
    nl,
    psi_hbm,
    left_hbm,
    right_hbm,
    left_order_hbm,
    right_order_hbm,
    left_qn_hbm,
    right_qn_hbm,
    left_dims_hbm,
    right_dims_hbm,
    first_ref,
    second_ref,
    psi,
    left_order,
    right_order,
    left_qn,
    right_qn,
    left_dims,
    right_dims,
    lsem,
    rbuf,
    lbuf,
    start,
    terms,
    sigma,
    landed,
    lsend,
    lrecv,
    zsend,
    zrecv,
    xsend,
    xrecv,
    ysend,
    yrecv,
    dsend,
    drecv,
    csend,
    crecv,
    ssend,
    srecv,
):
    l = lax.axis_index("lsec")
    z = lax.axis_index("rsec")
    o = lax.axis_index("ops")
    xp = (l + 2) % nl
    cp = l + 1 - 2 * (l % 2)
    op = 1 - o
    me = l * nz + z
    slots = nl * nz
    width = psi.shape[-1]
    kdev = lbuf.shape[1]
    to_y = {"ops": op}
    to_x = {"lsec": xp}
    to_c = {"lsec": cp}
    sent = []

    def send(src, dst, send_sem, recv_sem, where):
        copy = pltpu.make_async_remote_copy(
            src_ref=src,
            dst_ref=dst,
            send_sem=send_sem,
            recv_sem=recv_sem,
            device_id=where,
            device_id_type=MESH,
        )
        copy.start()
        sent.append(copy)

    def arrive(ref, sem):
        pltpu.make_async_copy(ref, ref, sem).wait()

    loads = [
        pltpu.make_async_copy(src, dst, lsem.at[i])
        for i, (src, dst) in enumerate(
            (
                (right_hbm.at[:, 0], rbuf.at[o, me]),
                (left_hbm.at[:, 0], lbuf.at[o]),
                (left_order_hbm, left_order),
                (right_order_hbm, right_order),
                (left_qn_hbm, left_qn),
                (right_qn_hbm, right_qn),
                (left_dims_hbm, left_dims),
                (right_dims_hbm, right_dims),
                (psi_hbm.at[0], psi),
            )
        )
    ]
    for load in loads:
        load.start()

    barrier = pltpu.get_barrier_semaphore()
    for s in range(nz):
        for t in range(nl):
            if s or t:
                pl.semaphore_signal(
                    barrier,
                    inc=1,
                    device_id={"lsec": (l + t) % nl, "rsec": (z + s) % nz},
                    device_id_type=MESH,
                )
    pl.semaphore_signal(barrier, inc=1, device_id=to_y, device_id_type=MESH)
    pl.semaphore_wait(barrier, slots)

    def slot_of(lane, s):
        return lane * nz + (z + s) % nz

    loads[0].wait()

    def stage_one(s):
        if s:
            arrive(rbuf.at[o, slot_of(l, s)], zrecv.at[s])
        piece = rbuf.at[o, slot_of(l, s)]
        send(piece, piece, ysend.at[s], yrecv.at[s], to_y)
        send(piece, piece, xsend.at[s], xrecv.at[s], to_x)
        send(piece, piece, csend.at[0, s], crecv.at[0, s], to_c)

    def stage_two(s):
        from_x = rbuf.at[o, slot_of(xp, s)]
        arrive(from_x, xrecv.at[s])
        half = rbuf.at[o, slot_of(xp, s), 0]
        send(half, half, dsend.at[0, s], drecv.at[0, s], to_y)
        send(from_x, from_x, csend.at[1, s], crecv.at[1, s], to_c)
        from_y = rbuf.at[op, slot_of(l, s)]
        arrive(from_y, yrecv.at[s])
        rest = rbuf.at[op, slot_of(l, s), pl.ds(1, kdev - 1)]
        send(rest, rest, dsend.at[1, s], drecv.at[1, s], to_x)
        send(from_y, from_y, csend.at[2, s], crecv.at[2, s], to_c)

    def stage_three(s):
        piece = rbuf.at[op, slot_of(xp, s)]
        arrive(rbuf.at[op, slot_of(xp, s), 0], drecv.at[0, s])
        arrive(rbuf.at[op, slot_of(xp, s), pl.ds(1, kdev - 1)], drecv.at[1, s])
        send(piece, piece, csend.at[3, s], crecv.at[3, s], to_c)

    def stage_four(s):
        cx = (cp + 2) % nl
        arrive(rbuf.at[o, slot_of(cp, s)], crecv.at[0, s])
        arrive(rbuf.at[o, slot_of(cx, s)], crecv.at[1, s])
        arrive(rbuf.at[op, slot_of(cp, s)], crecv.at[2, s])
        arrive(rbuf.at[op, slot_of(cx, s)], crecv.at[3, s])

    for s in range(1, nz):
        piece = rbuf.at[o, me]
        send(piece, piece, zsend.at[s], zrecv.at[s], {"rsec": (z + nz - s) % nz})
    stage_one(0)
    loads[1].wait()
    send(lbuf.at[o], lbuf.at[o], lsend, lrecv, to_y)
    for load in loads[2:]:
        load.wait()

    sector = left_order[me]
    my_qn = left_qn[sector]
    rows = lax.broadcasted_iota(jnp.int32, (width, width), 0)
    cols = lax.broadcasted_iota(jnp.int32, (width, width), 1)
    rows_used = rows < left_dims[sector]

    def masked(value, b):
        used = jnp.where(jnp.abs(my_qn - right_qn[b]) <= SPREAD, right_dims[b], 0)
        return jnp.where(rows_used & (cols < used), value, 0.0).astype(jnp.bfloat16)

    def start_pair(pair, carry):
        blocks = []
        for j in (2 * pair, 2 * pair + 1):
            b = right_order[j]
            blocks.append(masked(psi[b].astype(jnp.float32), b))
        start[pair] = jnp.concatenate(blocks, axis=1)
        return carry

    def terms_pair(pair, carry):
        for h in range(2):
            both = jnp.dot(
                lbuf[h].reshape(kdev * width, width),
                start[pair],
                preferred_element_type=jnp.float32,
            )
            both = both.astype(jnp.bfloat16).reshape(kdev, width, 2 * width)
            terms[2 * pair, h] = both[:, :, :width]
            terms[2 * pair + 1, h] = both[:, :, width:]
        return carry

    lax.fori_loop(0, slots // 2, start_pair, 0, unroll=2)
    arrive(lbuf.at[op], lrecv)
    stage_one(1)
    lax.fori_loop(0, slots // 2, terms_pair, 0, unroll=2)
    stage_two(0)

    def lanes(ref, j):
        return jnp.concatenate([ref[j, h, k] for h in range(2) for k in range(kdev)], axis=1)

    def right_lanes(j):
        return jnp.concatenate([rbuf[h, j, k] for h in range(2) for k in range(kdev)], axis=1)

    def first_blocks(s):
        for t in range(nl):
            j = slot_of((l + t) % nl, s)
            value = lax.dot_general(
                lanes(terms, j), right_lanes(j), NT, preferred_element_type=jnp.float32
            )
            sigma[j] = masked(value, right_order[j])
        for t in range(nl):
            j = slot_of((l + t) % nl, s)
            if s or t:
                send(
                    sigma.at[j],
                    landed.at[me],
                    ssend.at[s, t],
                    srecv.at[s, t],
                    {"lsec": (l + t) % nl, "rsec": (z + s) % nz},
                )
            else:
                landed[me] = sigma[j]

    for step in range(2, nz + 3):
        if step < nz:
            stage_one(step)
        if 1 <= step - 1 < nz:
            stage_two(step - 1)
        if 0 <= step - 2 < nz:
            stage_three(step - 2)
        if 0 <= step - 3 < nz:
            stage_four(step - 3)
            first_blocks(step - 3)

    def slot_holding(order, wanted):
        found = jnp.int32(0)
        for j in range(slots):
            found = jnp.where(order[j] == wanted, j, found)
        return found

    count = second_ref.shape[1]

    left_wide = jnp.concatenate([lbuf[h, k] for h in range(2) for k in range(kdev)], axis=1)

    def second_pair(i, carry):
        inner = []
        for n in range(2):
            j = slot_holding(right_order, o * count + 2 * i + n)
            halves = []
            for h in range(2):
                part = lax.dot_general(
                    sigma[j],
                    rbuf[h, j].reshape(kdev * width, width),
                    NT,
                    preferred_element_type=jnp.float32,
                ).astype(jnp.bfloat16)
                halves += [part[:, k * width : (k + 1) * width] for k in range(kdev)]
            inner.append(jnp.concatenate(halves, axis=0))
        both = jnp.dot(
            left_wide, jnp.concatenate(inner, axis=1), preferred_element_type=jnp.float32
        )
        for n in range(2):
            second_ref[0, 2 * i + n] = masked(
                both[:, n * width : (n + 1) * width], o * count + 2 * i + n
            )
        return carry

    lax.fori_loop(0, count // 2, second_pair, 0)

    for s in range(nz):
        for t in range(nl):
            if s or t:
                source = ((l + nl - t) % nl) * nz + (z + nz - s) % nz
                arrive(landed.at[source], srecv.at[s, t])

    def place(a, carry):
        first_ref[0, a] = landed[slot_holding(left_order, a)]
        return carry

    lax.fori_loop(0, slots, place, 0)

    for copy in sent:
        copy.wait_send()


def by_kernel(nz, nl, psi, left_ops, right_ops, *tables):
    slots = nl * nz
    width = psi.shape[-1]
    kdev = left_ops.shape[0]
    block = (width, width)
    dma = pltpu.SemaphoreType.DMA
    bf16 = jnp.bfloat16
    vmem = pl.BlockSpec(memory_space=pltpu.VMEM)
    hbm = pl.BlockSpec(memory_space=pltpu.HBM)
    flops = 2 * width**3 * 2 * kdev * slots * 3
    return pl.pallas_call(
        functools.partial(kernel, nz, nl),
        out_shape=(
            jax.ShapeDtypeStruct((1, slots) + block, bf16),
            jax.ShapeDtypeStruct((1, slots // 2) + block, bf16),
        ),
        in_specs=[hbm] * 9,
        out_specs=(vmem, vmem),
        scratch_shapes=[
            pltpu.VMEM((slots,) + block, bf16),
            *[pltpu.SMEM(table.shape, jnp.int32) for table in tables],
            dma((9,)),
            pltpu.VMEM((2, slots, kdev) + block, bf16),
            pltpu.VMEM((2, kdev) + block, bf16),
            pltpu.VMEM((slots // 2, width, 2 * width), bf16),
            pltpu.VMEM((slots, 2, kdev) + block, bf16),
            pltpu.VMEM((slots,) + block, bf16),
            pltpu.VMEM((slots,) + block, bf16),
            dma,
            dma,
            dma((nz,)),
            dma((nz,)),
            dma((nz,)),
            dma((nz,)),
            dma((nz,)),
            dma((nz,)),
            dma((2, nz)),
            dma((2, nz)),
            dma((4, nz)),
            dma((4, nz)),
            dma((nz, nl)),
            dma((nz, nl)),
        ],
        compiler_params=pltpu.CompilerParams(
            collective_id=0, has_side_effects=True, vmem_limit_bytes=56 * 2**20
        ),
        cost_estimate=pl.CostEstimate(flops=flops, bytes_accessed=4 * 2**20, transcendentals=0),
    )(psi, left_ops, right_ops, *tables)


def solution(mesh):
    nl, nz, no = mesh.shape["lsec"], mesh.shape["rsec"], mesh.shape["ops"]

    def on_device(psi, left_ops, right_ops, *tables):
        gathered = no * nl * nz * left_ops.size * left_ops.dtype.itemsize
        if no == 2 and nl == 4 and nz > 1 and left_ops.shape[0] > 1 and 3 * gathered <= VMEM_BUDGET:
            return by_kernel(nz, nl, psi, left_ops, right_ops, *tables)
        return by_collectives(psi, left_ops, right_ops, *tables)

    placed = (
        P(("lsec", "rsec"), None, None, None),
        P("ops", ("lsec", "rsec"), None, None),
        P("ops", ("lsec", "rsec"), None, None),
        P(),
        P(),
        P(),
        P(),
        P(),
        P(),
    )
    return jax.shard_map(
        on_device,
        mesh=mesh,
        in_specs=placed,
        out_specs=(P(("lsec", "rsec"), None, None, None), P(("lsec", "rsec"), "ops", None, None)),
        check_vma=False,
    )
```

```python
import functools

import jax
import jax.numpy as jnp
from jax import lax
from jax.experimental import pallas as pl
from jax.experimental.pallas import tpu as pltpu
from jax.sharding import PartitionSpec as P

SPREAD = 1
VMEM_BUDGET = 24 * 2**20
MESH = pl.DeviceIdType.MESH
NT = (((1,), (1,)), ((), ()))


def relayout(blocks):
    return lax.all_to_all(blocks, ("lsec", "rsec"), split_axis=1, concat_axis=1, tiled=True)


def inverse(order):
    count = order.shape[0]
    return jnp.zeros((count,), jnp.int32).at[order].set(jnp.arange(count, dtype=jnp.int32))


def by_collectives(
    psi, left_ops, right_ops, left_order, right_order, left_qn, right_qn, left_dims, right_dims
):
    slot = lax.axis_index(("lsec", "rsec"))
    width = psi.shape[-1]
    line = jnp.arange(width, dtype=jnp.int32)
    left_sector = left_order[slot]
    right_sector = right_order[slot]
    inv_left = inverse(left_order)
    inv_right = inverse(right_order)
    left_here = left_ops[:, 0]
    right_here = right_ops[:, 0]
    allowed_row = jnp.abs(left_qn[left_sector] - right_qn) <= SPREAD
    row_used = line < left_dims[left_sector]
    col_used = line[None, :] < right_dims[:, None]
    mask_left = allowed_row[:, None, None] & row_used[None, :, None] & col_used[:, None, :]
    allowed_col = jnp.abs(left_qn - right_qn[right_sector]) <= SPREAD
    rows_used = line[None, :] < left_dims[:, None]
    cols_here = line < right_dims[right_sector]
    mask_right = allowed_col[:, None, None] & rows_used[:, :, None] & cols_here[None, None, :]
    start = jnp.where(mask_left, psi[0], jnp.zeros((), jnp.bfloat16))
    start_slots = start[right_order]
    lefted = jnp.einsum(
        "kxy,byz->kbxz", left_here, start_slots, preferred_element_type=jnp.float32
    ).astype(jnp.bfloat16)
    arrived = relayout(lefted)
    partial_value = jnp.einsum(
        "kixy,kzy->ixz", arrived, right_here, preferred_element_type=jnp.float32
    )
    partial_value = partial_value[inv_left]
    summed = lax.psum(partial_value.astype(jnp.bfloat16), "ops").astype(jnp.float32)
    first = jnp.where(mask_right, summed, 0.0).astype(jnp.bfloat16)
    first_slots = first[left_order]
    righted = jnp.einsum(
        "ixy,kzy->kixz", first_slots, right_here, preferred_element_type=jnp.float32
    ).astype(jnp.bfloat16)
    returned = relayout(righted)
    second_partial = jnp.einsum(
        "kxy,kjyz->jxz", left_here, returned, preferred_element_type=jnp.float32
    )
    second_partial = second_partial[inv_right]
    second_share = lax.psum_scatter(
        second_partial.astype(jnp.bfloat16), "ops", scatter_dimension=0, tiled=True
    ).astype(jnp.float32)
    count = second_share.shape[0]
    mask_second = lax.dynamic_slice_in_dim(mask_left, lax.axis_index("ops") * count, count, 0)
    second = jnp.where(mask_second, second_share, 0.0).astype(jnp.bfloat16)
    return (first[None], second[None])


def kernel(
    nz,
    nl,
    psi_hbm,
    left_hbm,
    right_hbm,
    left_order_hbm,
    right_order_hbm,
    left_qn_hbm,
    right_qn_hbm,
    left_dims_hbm,
    right_dims_hbm,
    first_ref,
    second_ref,
    psi,
    left_order,
    right_order,
    left_qn,
    right_qn,
    left_dims,
    right_dims,
    lsem,
    rbuf,
    lbuf,
    start,
    terms,
    sigma,
    landed,
    lsend,
    lrecv,
    zsend,
    zrecv,
    xsend,
    xrecv,
    ysend,
    yrecv,
    dsend,
    drecv,
    csend,
    crecv,
    ssend,
    srecv,
    fsend,
    frecv,
    first,
    second,
    inverse_left,
    osem,
):
    l = lax.axis_index("lsec")
    z = lax.axis_index("rsec")
    o = lax.axis_index("ops")
    xp = (l + 2) % nl
    cp = l + 1 - 2 * (l % 2)
    op = 1 - o
    me = l * nz + z
    slots = nl * nz
    width = psi.shape[-1]
    kdev = lbuf.shape[1]
    to_y = {"ops": op}
    to_x = {"lsec": xp}
    to_c = {"lsec": cp}
    sent = []

    def send(src, dst, send_sem, recv_sem, where):
        copy = pltpu.make_async_remote_copy(
            src_ref=src,
            dst_ref=dst,
            send_sem=send_sem,
            recv_sem=recv_sem,
            device_id=where,
            device_id_type=MESH,
        )
        copy.start()
        sent.append(copy)

    def arrive(ref, sem):
        pltpu.make_async_copy(ref, ref, sem).wait()

    loads = [
        pltpu.make_async_copy(src, dst, lsem.at[i])
        for i, (src, dst) in enumerate(
            (
                (right_hbm.at[:, 0], rbuf.at[me, o]),
                (left_hbm.at[:, 0], lbuf.at[o]),
                (left_order_hbm, left_order),
                (right_order_hbm, right_order),
                (left_qn_hbm, left_qn),
                (right_qn_hbm, right_qn),
                (left_dims_hbm, left_dims),
                (right_dims_hbm, right_dims),
                (psi_hbm.at[0], psi),
            )
        )
    ]
    for load in loads:
        load.start()

    barrier = pltpu.get_barrier_semaphore()
    for s in range(nz):
        for t in range(nl):
            if s or t:
                pl.semaphore_signal(
                    barrier,
                    inc=1,
                    device_id={"lsec": (l + t) % nl, "rsec": (z + s) % nz},
                    device_id_type=MESH,
                )
    pl.semaphore_signal(barrier, inc=1, device_id=to_y, device_id_type=MESH)
    pl.semaphore_wait(barrier, slots)

    def slot_of(lane, s):
        return lane * nz + (z + s) % nz

    loads[0].wait()

    def stage_one(s):
        piece = rbuf.at[slot_of(l, s), o]
        if s:
            arrive(piece, zrecv.at[s])
        send(piece, piece, ysend.at[s], yrecv.at[s], to_y)
        send(piece, piece, xsend.at[s], xrecv.at[s], to_x)

    def stage_two(s):
        mine, theirs = slot_of(l, s), slot_of(xp, s)
        arrive(rbuf.at[theirs, o], xrecv.at[s])
        half = rbuf.at[theirs, o, 0]
        send(half, half, dsend.at[0, s], drecv.at[0, s], to_y)
        arrive(rbuf.at[mine, op], yrecv.at[s])
        rest = rbuf.at[mine, op, pl.ds(1, kdev - 1)]
        send(rest, rest, dsend.at[1, s], drecv.at[1, s], to_x)
        send(rbuf.at[mine], rbuf.at[mine], csend.at[0, s], crecv.at[0, s], to_c)

    def stage_three(s):
        theirs = slot_of(xp, s)
        arrive(rbuf.at[theirs, op, 0], drecv.at[0, s])
        arrive(rbuf.at[theirs, op, pl.ds(1, kdev - 1)], drecv.at[1, s])
        send(rbuf.at[theirs], rbuf.at[theirs], csend.at[1, s], crecv.at[1, s], to_c)

    def stage_four(s):
        arrive(rbuf.at[slot_of(cp, s)], crecv.at[0, s])
        arrive(rbuf.at[slot_of((cp + 2) % nl, s)], crecv.at[1, s])

    for s in range(1, nz):
        piece = rbuf.at[me, o]
        send(piece, piece, zsend.at[s], zrecv.at[s], {"rsec": (z + nz - s) % nz})
    stage_one(0)
    loads[1].wait()
    send(lbuf.at[o], lbuf.at[o], lsend, lrecv, to_y)
    for load in loads[2:]:
        load.wait()

    sector = left_order[me]
    my_qn = left_qn[sector]
    rows = lax.broadcasted_iota(jnp.int32, (width, width), 0)
    cols = lax.broadcasted_iota(jnp.int32, (width, width), 1)
    rows_used = rows < left_dims[sector]

    def masked(value, b):
        used = jnp.where(jnp.abs(my_qn - right_qn[b]) <= SPREAD, right_dims[b], 0)
        return jnp.where(rows_used & (cols < used), value, 0.0).astype(jnp.bfloat16)

    def start_pair(pair, carry):
        blocks = []
        for j in (2 * pair, 2 * pair + 1):
            b = right_order[j]
            blocks.append(masked(psi[b].astype(jnp.float32), b))
        start[pair] = jnp.concatenate(blocks, axis=1)
        return carry

    def terms_pair(pair, carry):
        for h in range(2):
            both = jnp.dot(
                lbuf[h].reshape(kdev * width, width),
                start[pair],
                preferred_element_type=jnp.float32,
            )
            both = both.astype(jnp.bfloat16).reshape(kdev, width, 2 * width)
            terms[2 * pair, h] = both[:, :, :width]
            terms[2 * pair + 1, h] = both[:, :, width:]
        return carry

    def lanes(ref, j):
        return jnp.concatenate([ref[j, h, k] for h in range(2) for k in range(kdev)], axis=1)

    def first_block(j):
        value = lax.dot_general(
            lanes(terms, j), lanes(rbuf, j), NT, preferred_element_type=jnp.float32
        )
        sigma[j] = masked(value, right_order[j])

    def direct(plane, s):
        if s == 0:
            return [1 + 2 * plane, 2]
        return [2 * u + (plane + s) % 2 for u in range(nl // 2)]

    def others(plane, s):
        if s == 0:
            return [0, 3 - 2 * plane]
        return [2 * u + (plane + s + 1) % 2 for u in range(nl // 2)]

    def relayed(s):
        return range(1 if s == 0 else nl // 2)

    def source_of(s, t):
        return ((l + nl - t) % nl) * nz + (z + nz - s) % nz

    def first_direct(s):
        targets = [(l + t) % nl for t in direct(o, s)]
        for there in targets:
            first_block(slot_of(there, s))
        for u, there in enumerate(targets):
            send(
                sigma.at[slot_of(there, s)],
                landed.at[me],
                ssend.at[s, u],
                srecv.at[s, u],
                {"lsec": there, "rsec": (z + s) % nz},
            )

    def relay(s):
        for u in relayed(s):
            block = landed.at[source_of(s, direct(o, s)[u])]
            arrive(block, srecv.at[s, u])
            send(block, block, fsend.at[s, u], frecv.at[s, u], to_y)

    lax.fori_loop(0, slots // 2, start_pair, 0, unroll=2)
    stage_one(1)
    stage_two(0)
    arrive(lbuf.at[op], lrecv)
    quarter = slots // 4
    lax.fori_loop(0, quarter, terms_pair, 0, unroll=2)
    for step in range(2, nz + 3):
        if step < nz:
            stage_one(step)
        if 1 <= step - 1 < nz:
            stage_two(step - 1)
        if 0 <= step - 2 < nz:
            stage_three(step - 2)
        if step == 2:
            lax.fori_loop(quarter, 2 * quarter, terms_pair, 0, unroll=2)
        if 0 <= step - 3 < nz:
            stage_four(step - 3)
            first_direct(step - 3)
        if 0 <= step - 5 < nz - 2:
            relay(step - 5)

    for s in range(nz):
        for t in others(o, s):
            first_block(slot_of((l + t) % nl, s))
    landed[me] = sigma[me]
    relay(nz - 2)

    def slot_holding(order, wanted):
        found = jnp.int32(0)
        for j in range(slots):
            found = jnp.where(order[j] == wanted, j, found)
        return found

    count = second_ref.shape[1]
    left_wide = jnp.concatenate([lbuf[h, k] for h in range(2) for k in range(kdev)], axis=1)

    def second_pair(i, carry):
        inner = []
        for n in range(2):
            j = slot_holding(right_order, o * count + 2 * i + n)
            halves = []
            for h in range(2):
                part = lax.dot_general(
                    sigma[j],
                    rbuf[j, h].reshape(kdev * width, width),
                    NT,
                    preferred_element_type=jnp.float32,
                ).astype(jnp.bfloat16)
                halves += [part[:, k * width : (k + 1) * width] for k in range(kdev)]
            inner.append(jnp.concatenate(halves, axis=0))
        both = jnp.dot(
            left_wide, jnp.concatenate(inner, axis=1), preferred_element_type=jnp.float32
        )
        for n in range(2):
            second[2 * i + n] = masked(
                both[:, n * width : (n + 1) * width], o * count + 2 * i + n
            )
        return carry

    lax.fori_loop(0, count // 4, second_pair, 0)
    relay(nz - 1)
    lax.fori_loop(count // 4, count // 2, second_pair, 0)
    out_second = pltpu.make_async_copy(second, second_ref.at[0], osem.at[0])
    out_second.start()

    def find(a, carry):
        inverse_left[a] = slot_holding(left_order, a)
        return carry

    lax.fori_loop(0, slots, find, 0)

    arrive(landed.at[source_of(0, 2)], srecv.at[0, 1])
    for s in range(nz):
        for u in relayed(s):
            arrive(landed.at[source_of(s, direct(op, s)[u])], frecv.at[s, u])

    def place(a, carry):
        first[a] = landed[inverse_left[a]]
        return carry

    lax.fori_loop(0, slots, place, 0, unroll=4)
    out_first = pltpu.make_async_copy(first, first_ref.at[0], osem.at[1])
    out_first.start()
    for copy in sent:
        copy.wait_send()
    out_second.wait()
    out_first.wait()


def hand_over(parts, *refs):
    count = len(refs) // 3
    copies = []
    for src, dst, sem in zip(refs[:count], refs[count : 2 * count], refs[2 * count :]):
        size = src.shape[1] // parts
        for i in range(parts):
            rows = pl.ds(i * size, size)
            copies.append(pltpu.make_async_copy(src.at[:, rows], dst.at[:, rows], sem.at[i]))
    for copy in copies:
        copy.start()
    for copy in copies:
        copy.wait()


def by_kernel(nz, nl, psi, left_ops, right_ops, *tables):
    slots = nl * nz
    width = psi.shape[-1]
    kdev = left_ops.shape[0]
    block = (width, width)
    dma = pltpu.SemaphoreType.DMA
    bf16 = jnp.bfloat16
    hbm = pl.BlockSpec(memory_space=pltpu.HBM)
    flops = 2 * width**3 * 2 * kdev * slots * 3
    shapes = (
        jax.ShapeDtypeStruct((1, slots) + block, bf16),
        jax.ShapeDtypeStruct((1, slots // 2) + block, bf16),
    )
    results = pl.pallas_call(
        functools.partial(kernel, nz, nl),
        out_shape=shapes,
        in_specs=[hbm] * 9,
        out_specs=(hbm, hbm),
        scratch_shapes=[
            pltpu.VMEM((slots,) + block, bf16),
            *[pltpu.SMEM(table.shape, jnp.int32) for table in tables],
            dma((9,)),
            pltpu.VMEM((slots, 2, kdev) + block, bf16),
            pltpu.VMEM((2, kdev) + block, bf16),
            pltpu.VMEM((slots // 2, width, 2 * width), bf16),
            pltpu.VMEM((slots, 2, kdev) + block, bf16),
            pltpu.VMEM((slots,) + block, bf16),
            pltpu.VMEM((slots,) + block, bf16),
            dma,
            dma,
            dma((nz,)),
            dma((nz,)),
            dma((nz,)),
            dma((nz,)),
            dma((nz,)),
            dma((nz,)),
            dma((2, nz)),
            dma((2, nz)),
            dma((2, nz)),
            dma((2, nz)),
            dma((nz, nl // 2)),
            dma((nz, nl // 2)),
            dma((nz, nl // 2)),
            dma((nz, nl // 2)),
            pltpu.VMEM((slots,) + block, bf16),
            pltpu.VMEM((slots // 2,) + block, bf16),
            pltpu.SMEM((slots,), jnp.int32),
            dma((2,)),
        ],
        compiler_params=pltpu.CompilerParams(
            collective_id=0, has_side_effects=True, vmem_limit_bytes=56 * 2**20
        ),
        cost_estimate=pl.CostEstimate(flops=flops, bytes_accessed=4 * 2**20, transcendentals=0),
    )(psi, left_ops, right_ops, *tables)
    parts = 4
    return pl.pallas_call(
        functools.partial(hand_over, parts),
        out_shape=shapes,
        in_specs=[hbm] * 2,
        out_specs=(hbm, hbm),
        scratch_shapes=[dma((parts,)), dma((parts,))],
        compiler_params=pltpu.CompilerParams(vmem_limit_bytes=56 * 2**20),
    )(*results)


def solution(mesh):
    nl, nz, no = mesh.shape["lsec"], mesh.shape["rsec"], mesh.shape["ops"]

    def on_device(psi, left_ops, right_ops, *tables):
        gathered = no * nl * nz * left_ops.size * left_ops.dtype.itemsize
        if no == 2 and nl == 4 and nz > 2 and left_ops.shape[0] > 1 and 3 * gathered <= VMEM_BUDGET:
            return by_kernel(nz, nl, psi, left_ops, right_ops, *tables)
        return by_collectives(psi, left_ops, right_ops, *tables)

    placed = (
        P(("lsec", "rsec"), None, None, None),
        P("ops", ("lsec", "rsec"), None, None),
        P("ops", ("lsec", "rsec"), None, None),
        P(),
        P(),
        P(),
        P(),
        P(),
        P(),
    )
    return jax.shard_map(
        on_device,
        mesh=mesh,
        in_specs=placed,
        out_specs=(P(("lsec", "rsec"), None, None, None), P(("lsec", "rsec"), "ops", None, None)),
        check_vma=False,
    )
```

```python
import functools

import jax
import jax.numpy as jnp
from jax import lax
from jax.experimental import pallas as pl
from jax.experimental.pallas import tpu as pltpu
from jax.sharding import PartitionSpec as P

SPREAD = 1
VMEM_BUDGET = 24 * 2**20
MESH = pl.DeviceIdType.MESH
NT = (((1,), (1,)), ((), ()))


def relayout(blocks):
    return lax.all_to_all(blocks, ("lsec", "rsec"), split_axis=1, concat_axis=1, tiled=True)


def inverse(order):
    count = order.shape[0]
    return jnp.zeros((count,), jnp.int32).at[order].set(jnp.arange(count, dtype=jnp.int32))


def by_collectives(
    psi, left_ops, right_ops, left_order, right_order, left_qn, right_qn, left_dims, right_dims
):
    slot = lax.axis_index(("lsec", "rsec"))
    width = psi.shape[-1]
    line = jnp.arange(width, dtype=jnp.int32)
    left_sector = left_order[slot]
    right_sector = right_order[slot]
    inv_left = inverse(left_order)
    inv_right = inverse(right_order)
    left_here = left_ops[:, 0]
    right_here = right_ops[:, 0]
    allowed_row = jnp.abs(left_qn[left_sector] - right_qn) <= SPREAD
    row_used = line < left_dims[left_sector]
    col_used = line[None, :] < right_dims[:, None]
    mask_left = allowed_row[:, None, None] & row_used[None, :, None] & col_used[:, None, :]
    allowed_col = jnp.abs(left_qn - right_qn[right_sector]) <= SPREAD
    rows_used = line[None, :] < left_dims[:, None]
    cols_here = line < right_dims[right_sector]
    mask_right = allowed_col[:, None, None] & rows_used[:, :, None] & cols_here[None, None, :]
    start = jnp.where(mask_left, psi[0], jnp.zeros((), jnp.bfloat16))
    start_slots = start[right_order]
    lefted = jnp.einsum(
        "kxy,byz->kbxz", left_here, start_slots, preferred_element_type=jnp.float32
    ).astype(jnp.bfloat16)
    arrived = relayout(lefted)
    partial_value = jnp.einsum(
        "kixy,kzy->ixz", arrived, right_here, preferred_element_type=jnp.float32
    )
    partial_value = partial_value[inv_left]
    summed = lax.psum(partial_value.astype(jnp.bfloat16), "ops").astype(jnp.float32)
    first = jnp.where(mask_right, summed, 0.0).astype(jnp.bfloat16)
    first_slots = first[left_order]
    righted = jnp.einsum(
        "ixy,kzy->kixz", first_slots, right_here, preferred_element_type=jnp.float32
    ).astype(jnp.bfloat16)
    returned = relayout(righted)
    second_partial = jnp.einsum(
        "kxy,kjyz->jxz", left_here, returned, preferred_element_type=jnp.float32
    )
    second_partial = second_partial[inv_right]
    second_share = lax.psum_scatter(
        second_partial.astype(jnp.bfloat16), "ops", scatter_dimension=0, tiled=True
    ).astype(jnp.float32)
    count = second_share.shape[0]
    mask_second = lax.dynamic_slice_in_dim(mask_left, lax.axis_index("ops") * count, count, 0)
    second = jnp.where(mask_second, second_share, 0.0).astype(jnp.bfloat16)
    return (first[None], second[None])


def kernel(
    nz,
    nl,
    psi_hbm,
    left_hbm,
    right_hbm,
    left_order_hbm,
    right_order_hbm,
    left_qn_hbm,
    right_qn_hbm,
    left_dims_hbm,
    right_dims_hbm,
    first_ref,
    second_ref,
    psi,
    left_order,
    right_order,
    left_qn,
    right_qn,
    left_dims,
    right_dims,
    lsem,
    rbuf,
    lbuf,
    start,
    terms,
    sigma,
    landed,
    lsend,
    lrecv,
    zsend,
    zrecv,
    xsend,
    xrecv,
    ysend,
    yrecv,
    dsend,
    drecv,
    csend,
    crecv,
    ssend,
    srecv,
    fsend,
    frecv,
    first,
    second,
    inverse_left,
    osem,
):
    l = lax.axis_index("lsec")
    z = lax.axis_index("rsec")
    o = lax.axis_index("ops")
    xp = (l + 2) % nl
    cp = l + 1 - 2 * (l % 2)
    op = 1 - o
    me = l * nz + z
    slots = nl * nz
    width = psi.shape[-1]
    kdev = lbuf.shape[1]
    to_y = {"ops": op}
    to_x = {"lsec": xp}
    to_c = {"lsec": cp}
    sent = []

    def send(src, dst, send_sem, recv_sem, where):
        copy = pltpu.make_async_remote_copy(
            src_ref=src,
            dst_ref=dst,
            send_sem=send_sem,
            recv_sem=recv_sem,
            device_id=where,
            device_id_type=MESH,
        )
        copy.start()
        sent.append(copy)

    def arrive(ref, sem):
        pltpu.make_async_copy(ref, ref, sem).wait()

    loads = [
        pltpu.make_async_copy(src, dst, lsem.at[i])
        for i, (src, dst) in enumerate(
            (
                (right_hbm.at[:, 0], rbuf.at[me, o]),
                (left_hbm.at[:, 0], lbuf.at[o]),
                (left_order_hbm, left_order),
                (right_order_hbm, right_order),
                (left_qn_hbm, left_qn),
                (right_qn_hbm, right_qn),
                (left_dims_hbm, left_dims),
                (right_dims_hbm, right_dims),
                (psi_hbm.at[0], psi),
            )
        )
    ]
    for load in loads:
        load.start()

    barrier = pltpu.get_barrier_semaphore()
    for s in range(nz):
        for t in range(nl):
            if s or t:
                pl.semaphore_signal(
                    barrier,
                    inc=1,
                    device_id={"lsec": (l + t) % nl, "rsec": (z + s) % nz},
                    device_id_type=MESH,
                )
    pl.semaphore_signal(barrier, inc=1, device_id=to_y, device_id_type=MESH)
    pl.semaphore_wait(barrier, slots)

    def slot_of(lane, s):
        return lane * nz + (z + s) % nz

    loads[0].wait()

    def stage_one(s):
        piece = rbuf.at[slot_of(l, s), o]
        if s:
            arrive(piece, zrecv.at[s])
        send(piece, piece, ysend.at[s], yrecv.at[s], to_y)
        send(piece, piece, xsend.at[s], xrecv.at[s], to_x)

    def stage_two(s):
        mine, theirs = slot_of(l, s), slot_of(xp, s)
        arrive(rbuf.at[theirs, o], xrecv.at[s])
        cut = 0 if s == 1 else 1
        if cut:
            half = rbuf.at[theirs, o, 0]
            send(half, half, dsend.at[0, s], drecv.at[0, s], to_y)
        arrive(rbuf.at[mine, op], yrecv.at[s])
        rest = rbuf.at[mine, op, pl.ds(cut, kdev - cut)]
        send(rest, rest, dsend.at[1, s], drecv.at[1, s], to_x)
        send(rbuf.at[mine], rbuf.at[mine], csend.at[0, s], crecv.at[0, s], to_c)

    def stage_three(s):
        theirs = slot_of(xp, s)
        cut = 0 if s == 1 else 1
        if cut:
            arrive(rbuf.at[theirs, op, 0], drecv.at[0, s])
        arrive(rbuf.at[theirs, op, pl.ds(cut, kdev - cut)], drecv.at[1, s])
        send(rbuf.at[theirs], rbuf.at[theirs], csend.at[1, s], crecv.at[1, s], to_c)

    def stage_four(s):
        arrive(rbuf.at[slot_of(cp, s)], crecv.at[0, s])
        arrive(rbuf.at[slot_of((cp + 2) % nl, s)], crecv.at[1, s])

    for s in range(1, nz):
        piece = rbuf.at[me, o]
        send(piece, piece, zsend.at[s], zrecv.at[s], {"rsec": (z + nz - s) % nz})
    stage_one(0)
    loads[1].wait()
    send(lbuf.at[o], lbuf.at[o], lsend, lrecv, to_y)
    for load in loads[2:]:
        load.wait()

    sector = left_order[me]
    my_qn = left_qn[sector]
    rows = lax.broadcasted_iota(jnp.int32, (width, width), 0)
    cols = lax.broadcasted_iota(jnp.int32, (width, width), 1)
    rows_used = rows < left_dims[sector]

    def masked(value, b):
        used = jnp.where(jnp.abs(my_qn - right_qn[b]) <= SPREAD, right_dims[b], 0)
        return jnp.where(rows_used & (cols < used), value, 0.0).astype(jnp.bfloat16)

    def start_pair(pair, carry):
        blocks = []
        for j in (2 * pair, 2 * pair + 1):
            b = right_order[j]
            blocks.append(masked(psi[b].astype(jnp.float32), b))
        start[pair] = jnp.concatenate(blocks, axis=1)
        return carry

    def terms_pair(pair, carry):
        for h in range(2):
            both = jnp.dot(
                lbuf[h].reshape(kdev * width, width),
                start[pair],
                preferred_element_type=jnp.float32,
            )
            both = both.astype(jnp.bfloat16).reshape(kdev, width, 2 * width)
            terms[2 * pair, h] = both[:, :, :width]
            terms[2 * pair + 1, h] = both[:, :, width:]
        return carry

    def lanes(ref, j):
        return jnp.concatenate([ref[j, h, k] for h in range(2) for k in range(kdev)], axis=1)

    def first_value(j, b):
        value = lax.dot_general(
            lanes(terms, j), lanes(rbuf, j), NT, preferred_element_type=jnp.float32
        )
        return masked(value, b)

    def first_block(j):
        sigma[j] = first_value(j, right_order[j])

    def direct(plane, s):
        if s == 0:
            return list(range(1, nl))
        return [2 * u + (plane + s) % 2 for u in range(nl // 2)]

    def source_of(s, t):
        return ((l + nl - t) % nl) * nz + (z + nz - s) % nz

    def first_direct(s):
        targets = [(l + t) % nl for t in direct(o, s)]
        for there in targets:
            first_block(slot_of(there, s))
        for u, there in enumerate(targets):
            send(
                sigma.at[slot_of(there, s)],
                landed.at[me],
                ssend.at[s, u],
                srecv.at[s, u],
                {"lsec": there, "rsec": (z + s) % nz},
            )

    def relay(s):
        for u in range(nl // 2):
            block = landed.at[source_of(s, direct(o, s)[u])]
            arrive(block, srecv.at[s, u])
            send(block, block, fsend.at[s, u], frecv.at[s, u], to_y)

    lax.fori_loop(0, slots // 2, start_pair, 0, unroll=2)
    stage_one(1)
    stage_two(0)
    arrive(lbuf.at[op], lrecv)
    def slot_holding(order, wanted):
        found = jnp.int32(0)
        for j in range(slots):
            found = jnp.where(order[j] == wanted, j, found)
        return found

    def find(a, carry):
        inverse_left[a] = slot_holding(left_order, a)
        return carry

    lax.fori_loop(0, slots, find, 0)
    quarter = slots // 4
    lax.fori_loop(0, quarter, terms_pair, 0, unroll=2)
    for step in range(2, nz + 3):
        if step < nz:
            stage_one(step)
        if 1 <= step - 1 < nz:
            stage_two(step - 1)
        if 0 <= step - 2 < nz:
            stage_three(step - 2)
        if step == 2:
            lax.fori_loop(quarter, 2 * quarter, terms_pair, 0, unroll=2)
        if 0 <= step - 3 < nz:
            stage_four(step - 3)
            first_direct(step - 3)
        if 0 < step - 5 < nz - 2:
            relay(step - 5)

    first_block(me)
    landed[me] = sigma[me]
    relay(nz - 2)

    count = second_ref.shape[1]
    left_wide = jnp.concatenate([lbuf[h, k] for h in range(2) for k in range(kdev)], axis=1)

    def second_pair(i, carry):
        inner = []
        for n in range(2):
            b = o * count + 2 * i + n
            j = slot_holding(right_order, b)
            state = first_value(j, b)
            halves = []
            for h in range(2):
                part = lax.dot_general(
                    state,
                    rbuf[j, h].reshape(kdev * width, width),
                    NT,
                    preferred_element_type=jnp.float32,
                ).astype(jnp.bfloat16)
                halves += [part[:, k * width : (k + 1) * width] for k in range(kdev)]
            inner.append(jnp.concatenate(halves, axis=0))
        both = jnp.dot(
            left_wide, jnp.concatenate(inner, axis=1), preferred_element_type=jnp.float32
        )
        for n in range(2):
            second[2 * i + n] = masked(
                both[:, n * width : (n + 1) * width], o * count + 2 * i + n
            )
        return carry

    lax.fori_loop(0, count // 4, second_pair, 0)
    relay(nz - 1)
    lax.fori_loop(count // 4, count // 2, second_pair, 0)
    out_second = pltpu.make_async_copy(second, second_ref.at[0], osem.at[0])
    out_second.start()

    for u, t in enumerate(direct(o, 0)):
        arrive(landed.at[source_of(0, t)], srecv.at[0, u])
    for s in range(1, nz):
        for u in range(nl // 2):
            arrive(landed.at[source_of(s, direct(op, s)[u])], frecv.at[s, u])

    def place(a, carry):
        first[a] = landed[inverse_left[a]]
        return carry

    lax.fori_loop(0, slots, place, 0, unroll=4)
    out_first = pltpu.make_async_copy(first, first_ref.at[0], osem.at[1])
    out_first.start()
    for copy in sent:
        copy.wait_send()
    out_second.wait()
    out_first.wait()


def hand_over(parts, first_in, second_in, first_out, second_out, first, second, sem):
    ins, outs = [], []
    for n, (src, mid, dst) in enumerate(
        ((second_in, second, second_out), (first_in, first, first_out))
    ):
        size = mid.shape[0] // parts
        for i in range(parts):
            rows = pl.ds(i * size, size)
            ins.append(pltpu.make_async_copy(src.at[0, rows], mid.at[rows], sem.at[0, n, i]))
            outs.append(pltpu.make_async_copy(mid.at[rows], dst.at[0, rows], sem.at[1, n, i]))
    for copy in ins:
        copy.start()
    for arrived, copy in zip(ins, outs):
        arrived.wait()
        copy.start()
    for copy in outs:
        copy.wait()


def by_kernel(nz, nl, psi, left_ops, right_ops, *tables):
    slots = nl * nz
    width = psi.shape[-1]
    kdev = left_ops.shape[0]
    block = (width, width)
    dma = pltpu.SemaphoreType.DMA
    bf16 = jnp.bfloat16
    hbm = pl.BlockSpec(memory_space=pltpu.HBM)
    flops = 2 * width**3 * 2 * kdev * slots * 3
    shapes = (
        jax.ShapeDtypeStruct((1, slots) + block, bf16),
        jax.ShapeDtypeStruct((1, slots // 2) + block, bf16),
    )
    results = pl.pallas_call(
        functools.partial(kernel, nz, nl),
        out_shape=shapes,
        in_specs=[hbm] * 9,
        out_specs=(hbm, hbm),
        scratch_shapes=[
            pltpu.VMEM((slots,) + block, bf16),
            *[pltpu.SMEM(table.shape, jnp.int32) for table in tables],
            dma((9,)),
            pltpu.VMEM((slots, 2, kdev) + block, bf16),
            pltpu.VMEM((2, kdev) + block, bf16),
            pltpu.VMEM((slots // 2, width, 2 * width), bf16),
            pltpu.VMEM((slots, 2, kdev) + block, bf16),
            pltpu.VMEM((slots,) + block, bf16),
            pltpu.VMEM((slots,) + block, bf16),
            dma,
            dma,
            dma((nz,)),
            dma((nz,)),
            dma((nz,)),
            dma((nz,)),
            dma((nz,)),
            dma((nz,)),
            dma((2, nz)),
            dma((2, nz)),
            dma((2, nz)),
            dma((2, nz)),
            dma((nz, nl)),
            dma((nz, nl)),
            dma((nz, nl // 2)),
            dma((nz, nl // 2)),
            pltpu.VMEM((slots,) + block, bf16),
            pltpu.VMEM((slots // 2,) + block, bf16),
            pltpu.SMEM((slots,), jnp.int32),
            dma((2,)),
        ],
        compiler_params=pltpu.CompilerParams(
            collective_id=0, has_side_effects=True, vmem_limit_bytes=56 * 2**20
        ),
        cost_estimate=pl.CostEstimate(flops=flops, bytes_accessed=4 * 2**20, transcendentals=0),
    )(psi, left_ops, right_ops, *tables)
    parts = 4
    return pl.pallas_call(
        functools.partial(hand_over, parts),
        out_shape=shapes,
        in_specs=[hbm] * 2,
        out_specs=(hbm, hbm),
        scratch_shapes=[
            pltpu.VMEM((slots,) + block, bf16),
            pltpu.VMEM((slots // 2,) + block, bf16),
            dma((2, 2, parts)),
        ],
        compiler_params=pltpu.CompilerParams(vmem_limit_bytes=56 * 2**20),
    )(*results)


def solution(mesh):
    nl, nz, no = mesh.shape["lsec"], mesh.shape["rsec"], mesh.shape["ops"]

    def on_device(psi, left_ops, right_ops, *tables):
        gathered = no * nl * nz * left_ops.size * left_ops.dtype.itemsize
        if no == 2 and nl == 4 and nz > 2 and left_ops.shape[0] > 1 and 3 * gathered <= VMEM_BUDGET:
            return by_kernel(nz, nl, psi, left_ops, right_ops, *tables)
        return by_collectives(psi, left_ops, right_ops, *tables)

    placed = (
        P(("lsec", "rsec"), None, None, None),
        P("ops", ("lsec", "rsec"), None, None),
        P("ops", ("lsec", "rsec"), None, None),
        P(),
        P(),
        P(),
        P(),
        P(),
        P(),
    )
    return jax.shard_map(
        on_device,
        mesh=mesh,
        in_specs=placed,
        out_specs=(P(("lsec", "rsec"), None, None, None), P(("lsec", "rsec"), "ops", None, None)),
        check_vma=False,
    )
```

```python
import functools

import jax
import jax.numpy as jnp
from jax import lax
from jax.experimental import pallas as pl
from jax.experimental.pallas import tpu as pltpu
from jax.sharding import PartitionSpec as P

SPREAD = 1
VMEM_BUDGET = 24 * 2**20
MESH = pl.DeviceIdType.MESH


def relayout(blocks):
    return lax.all_to_all(blocks, ("lsec", "rsec"), split_axis=1, concat_axis=1, tiled=True)


def inverse(order):
    count = order.shape[0]
    return jnp.zeros((count,), jnp.int32).at[order].set(jnp.arange(count, dtype=jnp.int32))


def by_collectives(
    psi, left_ops, right_ops, left_order, right_order, left_qn, right_qn, left_dims, right_dims
):
    slot = lax.axis_index(("lsec", "rsec"))
    width = psi.shape[-1]
    line = jnp.arange(width, dtype=jnp.int32)
    left_sector = left_order[slot]
    right_sector = right_order[slot]
    inv_left = inverse(left_order)
    inv_right = inverse(right_order)
    left_here = left_ops[:, 0]
    right_here = right_ops[:, 0]
    allowed_row = jnp.abs(left_qn[left_sector] - right_qn) <= SPREAD
    row_used = line < left_dims[left_sector]
    col_used = line[None, :] < right_dims[:, None]
    mask_left = allowed_row[:, None, None] & row_used[None, :, None] & col_used[:, None, :]
    allowed_col = jnp.abs(left_qn - right_qn[right_sector]) <= SPREAD
    rows_used = line[None, :] < left_dims[:, None]
    cols_here = line < right_dims[right_sector]
    mask_right = allowed_col[:, None, None] & rows_used[:, :, None] & cols_here[None, None, :]
    start = jnp.where(mask_left, psi[0], jnp.zeros((), jnp.bfloat16))
    start_slots = start[right_order]
    lefted = jnp.einsum(
        "kxy,byz->kbxz", left_here, start_slots, preferred_element_type=jnp.float32
    ).astype(jnp.bfloat16)
    arrived = relayout(lefted)
    partial_value = jnp.einsum(
        "kixy,kzy->ixz", arrived, right_here, preferred_element_type=jnp.float32
    )
    partial_value = partial_value[inv_left]
    summed = lax.psum(partial_value.astype(jnp.bfloat16), "ops").astype(jnp.float32)
    first = jnp.where(mask_right, summed, 0.0).astype(jnp.bfloat16)
    first_slots = first[left_order]
    righted = jnp.einsum(
        "ixy,kzy->kixz", first_slots, right_here, preferred_element_type=jnp.float32
    ).astype(jnp.bfloat16)
    returned = relayout(righted)
    second_partial = jnp.einsum(
        "kxy,kjyz->jxz", left_here, returned, preferred_element_type=jnp.float32
    )
    second_partial = second_partial[inv_right]
    second_share = lax.psum_scatter(
        second_partial.astype(jnp.bfloat16), "ops", scatter_dimension=0, tiled=True
    ).astype(jnp.float32)
    count = second_share.shape[0]
    mask_second = lax.dynamic_slice_in_dim(mask_left, lax.axis_index("ops") * count, count, 0)
    second = jnp.where(mask_second, second_share, 0.0).astype(jnp.bfloat16)
    return (first[None], second[None])


def kernel(
    nz,
    nl,
    psi_hbm,
    left_hbm,
    right_hbm,
    left_order_hbm,
    right_order_hbm,
    left_qn_hbm,
    right_qn_hbm,
    left_dims_hbm,
    right_dims_hbm,
    first_ref,
    second_ref,
    psi,
    left_order,
    right_order,
    left_qn,
    right_qn,
    left_dims,
    right_dims,
    right_own,
    lsem,
    rbuf,
    lbuf,
    start,
    terms,
    sigma,
    landed,
    lsend,
    lrecv,
    zsend,
    zrecv,
    xsend,
    xrecv,
    ysend,
    yrecv,
    dsend,
    drecv,
    csend,
    crecv,
    ssend,
    srecv,
    fsend,
    frecv,
    first,
    second,
    inverse_left,
    osem,
):
    l = lax.axis_index("lsec")
    z = lax.axis_index("rsec")
    o = lax.axis_index("ops")
    xp = (l + 2) % nl
    cp = l + 1 - 2 * (l % 2)
    op = 1 - o
    me = l * nz + z
    slots = nl * nz
    width = psi.shape[-1]
    kdev = lbuf.shape[1]
    to_y = {"ops": op}
    to_x = {"lsec": xp}
    to_c = {"lsec": cp}
    sent = []

    def send(src, dst, send_sem, recv_sem, where):
        copy = pltpu.make_async_remote_copy(
            src_ref=src,
            dst_ref=dst,
            send_sem=send_sem,
            recv_sem=recv_sem,
            device_id=where,
            device_id_type=MESH,
        )
        copy.start()
        sent.append(copy)

    def arrive(ref, sem):
        pltpu.make_async_copy(ref, ref, sem).wait()

    loads = [
        pltpu.make_async_copy(src, dst, lsem.at[i])
        for i, (src, dst) in enumerate(
            (
                (right_hbm.at[:, 0], right_own),
                (left_hbm.at[:, 0], lbuf.at[o]),
                (left_order_hbm, left_order),
                (right_order_hbm, right_order),
                (left_qn_hbm, left_qn),
                (right_qn_hbm, right_qn),
                (left_dims_hbm, left_dims),
                (right_dims_hbm, right_dims),
                (psi_hbm.at[0], psi),
            )
        )
    ]
    for load in loads:
        load.start()

    barrier = pltpu.get_barrier_semaphore()
    for s in range(nz):
        for t in range(nl):
            if s or t:
                pl.semaphore_signal(
                    barrier,
                    inc=1,
                    device_id={"lsec": (l + t) % nl, "rsec": (z + s) % nz},
                    device_id_type=MESH,
                )
    pl.semaphore_signal(barrier, inc=1, device_id=to_y, device_id_type=MESH)
    loads[0].wait()
    for k in range(kdev):
        rbuf[me, o, k] = right_own[k].astype(jnp.float32).T.astype(jnp.bfloat16)
    pl.semaphore_wait(barrier, slots)

    def slot_of(lane, s):
        return lane * nz + (z + s) % nz

    def stage_one(s):
        piece = rbuf.at[slot_of(l, s), o]
        if s:
            arrive(piece, zrecv.at[s])
        send(piece, piece, ysend.at[s], yrecv.at[s], to_y)
        send(piece, piece, xsend.at[s], xrecv.at[s], to_x)

    def stage_two(s):
        mine, theirs = slot_of(l, s), slot_of(xp, s)
        arrive(rbuf.at[theirs, o], xrecv.at[s])
        cut = 0 if s == 1 else 1
        if cut:
            half = rbuf.at[theirs, o, 0]
            send(half, half, dsend.at[0, s], drecv.at[0, s], to_y)
        arrive(rbuf.at[mine, op], yrecv.at[s])
        rest = rbuf.at[mine, op, pl.ds(cut, kdev - cut)]
        send(rest, rest, dsend.at[1, s], drecv.at[1, s], to_x)
        send(rbuf.at[mine], rbuf.at[mine], csend.at[0, s], crecv.at[0, s], to_c)

    def stage_three(s):
        theirs = slot_of(xp, s)
        cut = 0 if s == 1 else 1
        if cut:
            arrive(rbuf.at[theirs, op, 0], drecv.at[0, s])
        arrive(rbuf.at[theirs, op, pl.ds(cut, kdev - cut)], drecv.at[1, s])
        send(rbuf.at[theirs], rbuf.at[theirs], csend.at[1, s], crecv.at[1, s], to_c)

    def stage_four(s):
        arrive(rbuf.at[slot_of(cp, s)], crecv.at[0, s])
        arrive(rbuf.at[slot_of((cp + 2) % nl, s)], crecv.at[1, s])

    for s in range(1, nz):
        piece = rbuf.at[me, o]
        send(piece, piece, zsend.at[s], zrecv.at[s], {"rsec": (z + nz - s) % nz})
    stage_one(0)
    loads[1].wait()
    send(lbuf.at[o], lbuf.at[o], lsend, lrecv, to_y)
    for load in loads[2:]:
        load.wait()

    sector = left_order[me]
    my_qn = left_qn[sector]
    rows = lax.broadcasted_iota(jnp.int32, (width, width), 0)
    cols = lax.broadcasted_iota(jnp.int32, (width, width), 1)
    rows_used = rows < left_dims[sector]

    def masked(value, b):
        used = jnp.where(jnp.abs(my_qn - right_qn[b]) <= SPREAD, right_dims[b], 0)
        return jnp.where(rows_used & (cols < used), value, 0.0).astype(jnp.bfloat16)

    def start_pair(pair, carry):
        blocks = []
        for j in (2 * pair, 2 * pair + 1):
            b = right_order[j]
            blocks.append(masked(psi[b].astype(jnp.float32), b))
        start[pair] = jnp.concatenate(blocks, axis=1)
        return carry

    def terms_pair(pair, carry):
        for h in range(2):
            both = jnp.dot(
                lbuf[h].reshape(kdev * width, width),
                start[pair],
                preferred_element_type=jnp.float32,
            )
            both = both.astype(jnp.bfloat16).reshape(kdev, width, 2 * width)
            terms[2 * pair, h] = both[:, :, :width]
            terms[2 * pair + 1, h] = both[:, :, width:]
        return carry

    def lanes(ref, j):
        return jnp.concatenate([ref[j, h, k] for h in range(2) for k in range(kdev)], axis=1)

    def first_value(j, b):
        value = jnp.dot(
            lanes(terms, j),
            rbuf[j].reshape(2 * kdev * width, width),
            preferred_element_type=jnp.float32,
        )
        return masked(value, b)

    def first_block(j):
        sigma[j] = first_value(j, right_order[j])

    def direct(plane, s):
        if s == 0:
            return list(range(1, nl))
        return [2 * u + (plane + s) % 2 for u in range(nl // 2)]

    def source_of(s, t):
        return ((l + nl - t) % nl) * nz + (z + nz - s) % nz

    def first_direct(s):
        targets = [(l + t) % nl for t in direct(o, s)]
        for there in targets:
            first_block(slot_of(there, s))
        for u, there in enumerate(targets):
            send(
                sigma.at[slot_of(there, s)],
                landed.at[me],
                ssend.at[s, u],
                srecv.at[s, u],
                {"lsec": there, "rsec": (z + s) % nz},
            )

    def relay(s):
        for u in range(nl // 2):
            block = landed.at[source_of(s, direct(o, s)[u])]
            arrive(block, srecv.at[s, u])
            send(block, block, fsend.at[s, u], frecv.at[s, u], to_y)

    lax.fori_loop(0, slots // 2, start_pair, 0, unroll=2)
    stage_one(1)
    stage_two(0)
    arrive(lbuf.at[op], lrecv)
    def slot_holding(order, wanted):
        found = jnp.int32(0)
        for j in range(slots):
            found = jnp.where(order[j] == wanted, j, found)
        return found

    def find(a, carry):
        inverse_left[a] = slot_holding(left_order, a)
        return carry

    lax.fori_loop(0, slots, find, 0)
    quarter = slots // 4
    lax.fori_loop(0, quarter, terms_pair, 0, unroll=2)
    for step in range(2, nz + 3):
        if step < nz:
            stage_one(step)
        if 1 <= step - 1 < nz:
            stage_two(step - 1)
        if 0 <= step - 2 < nz:
            stage_three(step - 2)
        if step == 2:
            lax.fori_loop(quarter, 2 * quarter, terms_pair, 0, unroll=2)
        if 0 <= step - 3 < nz:
            stage_four(step - 3)
            first_direct(step - 3)
        if 0 < step - 5 < nz - 2:
            relay(step - 5)

    first_block(me)
    landed[me] = sigma[me]
    relay(nz - 2)

    count = second_ref.shape[1]
    left_wide = jnp.concatenate([lbuf[h, k] for h in range(2) for k in range(kdev)], axis=1)

    def second_pair(i, carry):
        inner = []
        for n in range(2):
            b = o * count + 2 * i + n
            j = slot_holding(right_order, b)
            state = first_value(j, b)
            part = jnp.dot(state, lanes(rbuf, j), preferred_element_type=jnp.float32)
            part = part.astype(jnp.bfloat16)
            halves = [part[:, k * width : (k + 1) * width] for k in range(2 * kdev)]
            inner.append(jnp.concatenate(halves, axis=0))
        both = jnp.dot(
            left_wide, jnp.concatenate(inner, axis=1), preferred_element_type=jnp.float32
        )
        for n in range(2):
            second[2 * i + n] = masked(
                both[:, n * width : (n + 1) * width], o * count + 2 * i + n
            )
        return carry

    lax.fori_loop(0, count // 4, second_pair, 0)
    relay(nz - 1)
    lax.fori_loop(count // 4, count // 2, second_pair, 0)
    out_second = pltpu.make_async_copy(second, second_ref.at[0], osem.at[0])
    out_second.start()

    for u, t in enumerate(direct(o, 0)):
        arrive(landed.at[source_of(0, t)], srecv.at[0, u])
    for s in range(1, nz):
        for u in range(nl // 2):
            arrive(landed.at[source_of(s, direct(op, s)[u])], frecv.at[s, u])

    def place(a, carry):
        first[a] = landed[inverse_left[a]]
        return carry

    lax.fori_loop(0, slots, place, 0, unroll=4)
    out_first = pltpu.make_async_copy(first, first_ref.at[0], osem.at[1])
    out_first.start()
    for copy in sent:
        copy.wait_send()
    out_second.wait()
    out_first.wait()


def hand_over(parts, first_in, second_in, first_out, second_out, first, second, sem):
    ins, outs = [], []
    for n, (src, mid, dst) in enumerate(
        ((second_in, second, second_out), (first_in, first, first_out))
    ):
        size = mid.shape[0] // parts
        for i in range(parts):
            rows = pl.ds(i * size, size)
            ins.append(pltpu.make_async_copy(src.at[0, rows], mid.at[rows], sem.at[0, n, i]))
            outs.append(pltpu.make_async_copy(mid.at[rows], dst.at[0, rows], sem.at[1, n, i]))
    for copy in ins:
        copy.start()
    for arrived, copy in zip(ins, outs):
        arrived.wait()
        copy.start()
    for copy in outs:
        copy.wait()


def by_kernel(nz, nl, psi, left_ops, right_ops, *tables):
    slots = nl * nz
    width = psi.shape[-1]
    kdev = left_ops.shape[0]
    block = (width, width)
    dma = pltpu.SemaphoreType.DMA
    bf16 = jnp.bfloat16
    hbm = pl.BlockSpec(memory_space=pltpu.HBM)
    flops = 2 * width**3 * 2 * kdev * slots * 3
    shapes = (
        jax.ShapeDtypeStruct((1, slots) + block, bf16),
        jax.ShapeDtypeStruct((1, slots // 2) + block, bf16),
    )
    results = pl.pallas_call(
        functools.partial(kernel, nz, nl),
        out_shape=shapes,
        in_specs=[hbm] * 9,
        out_specs=(hbm, hbm),
        scratch_shapes=[
            pltpu.VMEM((slots,) + block, bf16),
            *[pltpu.SMEM(table.shape, jnp.int32) for table in tables],
            pltpu.VMEM((kdev,) + block, bf16),
            dma((9,)),
            pltpu.VMEM((slots, 2, kdev) + block, bf16),
            pltpu.VMEM((2, kdev) + block, bf16),
            pltpu.VMEM((slots // 2, width, 2 * width), bf16),
            pltpu.VMEM((slots, 2, kdev) + block, bf16),
            pltpu.VMEM((slots,) + block, bf16),
            pltpu.VMEM((slots,) + block, bf16),
            dma,
            dma,
            dma((nz,)),
            dma((nz,)),
            dma((nz,)),
            dma((nz,)),
            dma((nz,)),
            dma((nz,)),
            dma((2, nz)),
            dma((2, nz)),
            dma((2, nz)),
            dma((2, nz)),
            dma((nz, nl)),
            dma((nz, nl)),
            dma((nz, nl // 2)),
            dma((nz, nl // 2)),
            pltpu.VMEM((slots,) + block, bf16),
            pltpu.VMEM((slots // 2,) + block, bf16),
            pltpu.SMEM((slots,), jnp.int32),
            dma((2,)),
        ],
        compiler_params=pltpu.CompilerParams(
            collective_id=0, has_side_effects=True, vmem_limit_bytes=56 * 2**20
        ),
        cost_estimate=pl.CostEstimate(flops=flops, bytes_accessed=4 * 2**20, transcendentals=0),
    )(psi, left_ops, right_ops, *tables)
    parts = 4
    return pl.pallas_call(
        functools.partial(hand_over, parts),
        out_shape=shapes,
        in_specs=[hbm] * 2,
        out_specs=(hbm, hbm),
        scratch_shapes=[
            pltpu.VMEM((slots,) + block, bf16),
            pltpu.VMEM((slots // 2,) + block, bf16),
            dma((2, 2, parts)),
        ],
        compiler_params=pltpu.CompilerParams(vmem_limit_bytes=56 * 2**20),
    )(*results)


def solution(mesh):
    nl, nz, no = mesh.shape["lsec"], mesh.shape["rsec"], mesh.shape["ops"]

    def on_device(psi, left_ops, right_ops, *tables):
        gathered = no * nl * nz * left_ops.size * left_ops.dtype.itemsize
        if no == 2 and nl == 4 and nz > 2 and left_ops.shape[0] > 1 and 3 * gathered <= VMEM_BUDGET:
            return by_kernel(nz, nl, psi, left_ops, right_ops, *tables)
        return by_collectives(psi, left_ops, right_ops, *tables)

    placed = (
        P(("lsec", "rsec"), None, None, None),
        P("ops", ("lsec", "rsec"), None, None),
        P("ops", ("lsec", "rsec"), None, None),
        P(),
        P(),
        P(),
        P(),
        P(),
        P(),
    )
    return jax.shard_map(
        on_device,
        mesh=mesh,
        in_specs=placed,
        out_specs=(P(("lsec", "rsec"), None, None, None), P(("lsec", "rsec"), "ops", None, None)),
        check_vma=False,
    )
```

```python
import functools

import jax
import jax.numpy as jnp
from jax import lax
from jax.experimental import pallas as pl
from jax.experimental.pallas import tpu as pltpu
from jax.sharding import PartitionSpec as P

SPREAD = 1
VMEM_BUDGET = 24 * 2**20
MESH = pl.DeviceIdType.MESH


def relayout(blocks):
    return lax.all_to_all(blocks, ("lsec", "rsec"), split_axis=1, concat_axis=1, tiled=True)


def inverse(order):
    count = order.shape[0]
    return jnp.zeros((count,), jnp.int32).at[order].set(jnp.arange(count, dtype=jnp.int32))


def by_collectives(
    psi, left_ops, right_ops, left_order, right_order, left_qn, right_qn, left_dims, right_dims
):
    slot = lax.axis_index(("lsec", "rsec"))
    width = psi.shape[-1]
    line = jnp.arange(width, dtype=jnp.int32)
    left_sector = left_order[slot]
    right_sector = right_order[slot]
    inv_left = inverse(left_order)
    inv_right = inverse(right_order)
    left_here = left_ops[:, 0]
    right_here = right_ops[:, 0]
    allowed_row = jnp.abs(left_qn[left_sector] - right_qn) <= SPREAD
    row_used = line < left_dims[left_sector]
    col_used = line[None, :] < right_dims[:, None]
    mask_left = allowed_row[:, None, None] & row_used[None, :, None] & col_used[:, None, :]
    allowed_col = jnp.abs(left_qn - right_qn[right_sector]) <= SPREAD
    rows_used = line[None, :] < left_dims[:, None]
    cols_here = line < right_dims[right_sector]
    mask_right = allowed_col[:, None, None] & rows_used[:, :, None] & cols_here[None, None, :]
    start = jnp.where(mask_left, psi[0], jnp.zeros((), jnp.bfloat16))
    start_slots = start[right_order]
    lefted = jnp.einsum(
        "kxy,byz->kbxz", left_here, start_slots, preferred_element_type=jnp.float32
    ).astype(jnp.bfloat16)
    arrived = relayout(lefted)
    partial_value = jnp.einsum(
        "kixy,kzy->ixz", arrived, right_here, preferred_element_type=jnp.float32
    )
    partial_value = partial_value[inv_left]
    summed = lax.psum(partial_value.astype(jnp.bfloat16), "ops").astype(jnp.float32)
    first = jnp.where(mask_right, summed, 0.0).astype(jnp.bfloat16)
    first_slots = first[left_order]
    righted = jnp.einsum(
        "ixy,kzy->kixz", first_slots, right_here, preferred_element_type=jnp.float32
    ).astype(jnp.bfloat16)
    returned = relayout(righted)
    second_partial = jnp.einsum(
        "kxy,kjyz->jxz", left_here, returned, preferred_element_type=jnp.float32
    )
    second_partial = second_partial[inv_right]
    second_share = lax.psum_scatter(
        second_partial.astype(jnp.bfloat16), "ops", scatter_dimension=0, tiled=True
    ).astype(jnp.float32)
    count = second_share.shape[0]
    mask_second = lax.dynamic_slice_in_dim(mask_left, lax.axis_index("ops") * count, count, 0)
    second = jnp.where(mask_second, second_share, 0.0).astype(jnp.bfloat16)
    return (first[None], second[None])


def kernel(
    nz,
    nl,
    psi_hbm,
    left_hbm,
    right_hbm,
    left_order_hbm,
    right_order_hbm,
    left_qn_hbm,
    right_qn_hbm,
    left_dims_hbm,
    right_dims_hbm,
    first_ref,
    second_ref,
    psi,
    left_order,
    right_order,
    left_qn,
    right_qn,
    left_dims,
    right_dims,
    right_own,
    lsem,
    rbuf,
    lbuf,
    start,
    terms,
    sigma,
    landed,
    lsend,
    lrecv,
    zsend,
    zrecv,
    xsend,
    xrecv,
    ysend,
    yrecv,
    dsend,
    drecv,
    csend,
    crecv,
    ssend,
    srecv,
    fsend,
    frecv,
    first,
    second,
    inverse_left,
    osem,
):
    l = lax.axis_index("lsec")
    z = lax.axis_index("rsec")
    o = lax.axis_index("ops")
    xp = (l + 2) % nl
    cp = l + 1 - 2 * (l % 2)
    op = 1 - o
    me = l * nz + z
    slots = nl * nz
    width = psi.shape[-1]
    kdev = lbuf.shape[1]
    to_y = {"ops": op}
    to_x = {"lsec": xp}
    to_c = {"lsec": cp}
    to_d = {"lsec": xp, "ops": op}
    sent = []

    def send(src, dst, send_sem, recv_sem, where):
        copy = pltpu.make_async_remote_copy(
            src_ref=src,
            dst_ref=dst,
            send_sem=send_sem,
            recv_sem=recv_sem,
            device_id=where,
            device_id_type=MESH,
        )
        copy.start()
        sent.append(copy)

    def arrive(ref, sem):
        pltpu.make_async_copy(ref, ref, sem).wait()

    loads = [
        pltpu.make_async_copy(src, dst, lsem.at[i])
        for i, (src, dst) in enumerate(
            (
                (right_hbm.at[:, 0], right_own),
                (left_hbm.at[:, 0], lbuf.at[o]),
                (left_order_hbm, left_order),
                (right_order_hbm, right_order),
                (left_qn_hbm, left_qn),
                (right_qn_hbm, right_qn),
                (left_dims_hbm, left_dims),
                (right_dims_hbm, right_dims),
                (psi_hbm.at[0], psi),
            )
        )
    ]
    for load in loads:
        load.start()

    barrier = pltpu.get_barrier_semaphore()
    for s in range(nz):
        for t in range(nl):
            if s or t:
                pl.semaphore_signal(
                    barrier,
                    inc=1,
                    device_id={"lsec": (l + t) % nl, "rsec": (z + s) % nz},
                    device_id_type=MESH,
                )
    for where in (to_y, to_d):
        pl.semaphore_signal(barrier, inc=1, device_id=where, device_id_type=MESH)
    loads[0].wait()
    for k in range(kdev):
        rbuf[me, o, k] = right_own[k].astype(jnp.float32).T.astype(jnp.bfloat16)
    pl.semaphore_wait(barrier, slots + 1)

    def slot_of(lane, s):
        return lane * nz + (z + s) % nz

    def stage_one(s):
        piece = rbuf.at[slot_of(l, s), o]
        if s:
            arrive(piece, zrecv.at[s])
        send(piece, piece, ysend.at[s], yrecv.at[s], to_y)
        send(piece, piece, xsend.at[s], xrecv.at[s], to_x)

        if s == nz - 1:
            send(piece, piece, dsend.at[0, s], drecv.at[0, s], to_d)

    def cut(s):
        return 0 if s == 1 else 1

    def stage_two(s):
        mine, theirs = slot_of(l, s), slot_of(xp, s)
        arrive(rbuf.at[theirs, o], xrecv.at[s])
        if s < nz - 1 and cut(s):
            half = rbuf.at[theirs, o, 0]
            send(half, half, dsend.at[0, s], drecv.at[0, s], to_y)
        arrive(rbuf.at[mine, op], yrecv.at[s])
        if s < nz - 1:
            rest = rbuf.at[mine, op, pl.ds(cut(s), kdev - cut(s))]
            send(rest, rest, dsend.at[1, s], drecv.at[1, s], to_x)
        send(rbuf.at[mine], rbuf.at[mine], csend.at[0, s], crecv.at[0, s], to_c)

    def stage_three(s):
        theirs = slot_of(xp, s)
        if s == nz - 1:
            arrive(rbuf.at[theirs, op], drecv.at[0, s])
        else:
            if cut(s):
                arrive(rbuf.at[theirs, op, 0], drecv.at[0, s])
            arrive(rbuf.at[theirs, op, pl.ds(cut(s), kdev - cut(s))], drecv.at[1, s])
        send(rbuf.at[theirs], rbuf.at[theirs], csend.at[1, s], crecv.at[1, s], to_c)

    def stage_four(s):
        arrive(rbuf.at[slot_of(cp, s)], crecv.at[0, s])
        arrive(rbuf.at[slot_of((cp + 2) % nl, s)], crecv.at[1, s])

    for s in range(1, nz):
        piece = rbuf.at[me, o]
        send(piece, piece, zsend.at[s], zrecv.at[s], {"rsec": (z + nz - s) % nz})
    stage_one(0)
    loads[1].wait()
    send(lbuf.at[o], lbuf.at[o], lsend, lrecv, to_y)
    for load in loads[2:]:
        load.wait()

    sector = left_order[me]
    my_qn = left_qn[sector]
    rows = lax.broadcasted_iota(jnp.int32, (width, width), 0)
    cols = lax.broadcasted_iota(jnp.int32, (width, width), 1)
    rows_used = rows < left_dims[sector]

    def masked(value, b):
        used = jnp.where(jnp.abs(my_qn - right_qn[b]) <= SPREAD, right_dims[b], 0)
        return jnp.where(rows_used & (cols < used), value, 0.0).astype(jnp.bfloat16)

    def start_pair(pair, carry):
        blocks = []
        for j in (2 * pair, 2 * pair + 1):
            b = right_order[j]
            blocks.append(masked(psi[b].astype(jnp.float32), b))
        start[pair] = jnp.concatenate(blocks, axis=1)
        return carry

    def terms_pair(pair, carry):
        for h in range(2):
            both = jnp.dot(
                lbuf[h].reshape(kdev * width, width),
                start[pair],
                preferred_element_type=jnp.float32,
            )
            both = both.astype(jnp.bfloat16).reshape(kdev, width, 2 * width)
            terms[2 * pair, h] = both[:, :, :width]
            terms[2 * pair + 1, h] = both[:, :, width:]
        return carry

    def lanes(ref, j):
        return jnp.concatenate([ref[j, h, k] for h in range(2) for k in range(kdev)], axis=1)

    def first_value(j, b):
        value = jnp.dot(
            lanes(terms, j),
            rbuf[j].reshape(2 * kdev * width, width),
            preferred_element_type=jnp.float32,
        )
        return masked(value, b)

    def first_block(j):
        sigma[j] = first_value(j, right_order[j])

    def direct(plane, s):
        if s == 0 or s == nz - 1:
            return list(range(0 if s else 1, nl))
        return [2 * u + (plane + s) % 2 for u in range(nl // 2)]

    def source_of(s, t):
        return ((l + nl - t) % nl) * nz + (z + nz - s) % nz

    def first_direct(s):
        targets = [(l + t) % nl for t in direct(o, s)]
        for there in targets:
            first_block(slot_of(there, s))
        for u, there in enumerate(targets):
            send(
                sigma.at[slot_of(there, s)],
                landed.at[me],
                ssend.at[s, u],
                srecv.at[s, u],
                {"lsec": there, "rsec": (z + s) % nz},
            )

    def relay(s):
        for u in range(nl // 2):
            block = landed.at[source_of(s, direct(o, s)[u])]
            arrive(block, srecv.at[s, u])
            send(block, block, fsend.at[s, u], frecv.at[s, u], to_y)

    lax.fori_loop(0, slots // 2, start_pair, 0, unroll=2)
    stage_one(1)
    stage_two(0)
    arrive(lbuf.at[op], lrecv)
    def slot_holding(order, wanted):
        found = jnp.int32(0)
        for j in range(slots):
            found = jnp.where(order[j] == wanted, j, found)
        return found

    def find(a, carry):
        inverse_left[a] = slot_holding(left_order, a)
        return carry

    lax.fori_loop(0, slots, find, 0)
    quarter = slots // 4
    lax.fori_loop(0, quarter, terms_pair, 0, unroll=2)
    for step in range(2, nz + 2):
        if step < nz:
            stage_one(step)
        if step - 1 < nz:
            stage_two(step - 1)
        if step - 2 < nz - 1:
            stage_three(step - 2)
        if step == nz:
            stage_three(nz - 1)
        if step == 2:
            lax.fori_loop(quarter, 2 * quarter, terms_pair, 0, unroll=2)
        if 0 <= step - 3:
            stage_four(step - 3)
            first_direct(step - 3)
    stage_four(nz - 1)
    first_direct(nz - 1)
    for s in range(1, nz - 2):
        relay(s)

    first_block(me)
    landed[me] = sigma[me]

    count = second_ref.shape[1]
    left_wide = jnp.concatenate([lbuf[h, k] for h in range(2) for k in range(kdev)], axis=1)

    def second_pair(i, carry):
        inner = []
        for n in range(2):
            b = o * count + 2 * i + n
            j = slot_holding(right_order, b)
            state = first_value(j, b)
            part = jnp.dot(state, lanes(rbuf, j), preferred_element_type=jnp.float32)
            part = part.astype(jnp.bfloat16)
            halves = [part[:, k * width : (k + 1) * width] for k in range(2 * kdev)]
            inner.append(jnp.concatenate(halves, axis=0))
        both = jnp.dot(
            left_wide, jnp.concatenate(inner, axis=1), preferred_element_type=jnp.float32
        )
        for n in range(2):
            second[2 * i + n] = masked(
                both[:, n * width : (n + 1) * width], o * count + 2 * i + n
            )
        return carry

    lax.fori_loop(0, count // 4, second_pair, 0)
    relay(nz - 2)
    lax.fori_loop(count // 4, count // 2, second_pair, 0)
    out_second = pltpu.make_async_copy(second, second_ref.at[0], osem.at[0])
    out_second.start()

    for s in (0, nz - 1):
        for u, t in enumerate(direct(o, s)):
            arrive(landed.at[source_of(s, t)], srecv.at[s, u])
    for s in range(1, nz - 1):
        for u in range(nl // 2):
            arrive(landed.at[source_of(s, direct(op, s)[u])], frecv.at[s, u])

    def place(a, carry):
        first[a] = landed[inverse_left[a]]
        return carry

    lax.fori_loop(0, slots, place, 0, unroll=4)
    out_first = pltpu.make_async_copy(first, first_ref.at[0], osem.at[1])
    out_first.start()
    for copy in sent:
        copy.wait_send()
    out_second.wait()
    out_first.wait()


def hand_over(parts, first_in, second_in, first_out, second_out, first, second, sem):
    ins, outs = [], []
    for n, (src, mid, dst) in enumerate(
        ((second_in, second, second_out), (first_in, first, first_out))
    ):
        size = mid.shape[0] // parts
        for i in range(parts):
            rows = pl.ds(i * size, size)
            ins.append(pltpu.make_async_copy(src.at[0, rows], mid.at[rows], sem.at[0, n, i]))
            outs.append(pltpu.make_async_copy(mid.at[rows], dst.at[0, rows], sem.at[1, n, i]))
    for copy in ins:
        copy.start()
    for arrived, copy in zip(ins, outs):
        arrived.wait()
        copy.start()
    for copy in outs:
        copy.wait()


def by_kernel(nz, nl, psi, left_ops, right_ops, *tables):
    slots = nl * nz
    width = psi.shape[-1]
    kdev = left_ops.shape[0]
    block = (width, width)
    dma = pltpu.SemaphoreType.DMA
    bf16 = jnp.bfloat16
    hbm = pl.BlockSpec(memory_space=pltpu.HBM)
    flops = 2 * width**3 * 2 * kdev * slots * 3
    shapes = (
        jax.ShapeDtypeStruct((1, slots) + block, bf16),
        jax.ShapeDtypeStruct((1, slots // 2) + block, bf16),
    )
    results = pl.pallas_call(
        functools.partial(kernel, nz, nl),
        out_shape=shapes,
        in_specs=[hbm] * 9,
        out_specs=(hbm, hbm),
        scratch_shapes=[
            pltpu.VMEM((slots,) + block, bf16),
            *[pltpu.SMEM(table.shape, jnp.int32) for table in tables],
            pltpu.VMEM((kdev,) + block, bf16),
            dma((9,)),
            pltpu.VMEM((slots, 2, kdev) + block, bf16),
            pltpu.VMEM((2, kdev) + block, bf16),
            pltpu.VMEM((slots // 2, width, 2 * width), bf16),
            pltpu.VMEM((slots, 2, kdev) + block, bf16),
            pltpu.VMEM((slots,) + block, bf16),
            pltpu.VMEM((slots,) + block, bf16),
            dma,
            dma,
            dma((nz,)),
            dma((nz,)),
            dma((nz,)),
            dma((nz,)),
            dma((nz,)),
            dma((nz,)),
            dma((2, nz)),
            dma((2, nz)),
            dma((2, nz)),
            dma((2, nz)),
            dma((nz, nl)),
            dma((nz, nl)),
            dma((nz, nl // 2)),
            dma((nz, nl // 2)),
            pltpu.VMEM((slots,) + block, bf16),
            pltpu.VMEM((slots // 2,) + block, bf16),
            pltpu.SMEM((slots,), jnp.int32),
            dma((2,)),
        ],
        compiler_params=pltpu.CompilerParams(
            collective_id=0, has_side_effects=True, vmem_limit_bytes=56 * 2**20
        ),
        cost_estimate=pl.CostEstimate(flops=flops, bytes_accessed=4 * 2**20, transcendentals=0),
    )(psi, left_ops, right_ops, *tables)
    parts = 4
    return pl.pallas_call(
        functools.partial(hand_over, parts),
        out_shape=shapes,
        in_specs=[hbm] * 2,
        out_specs=(hbm, hbm),
        scratch_shapes=[
            pltpu.VMEM((slots,) + block, bf16),
            pltpu.VMEM((slots // 2,) + block, bf16),
            dma((2, 2, parts)),
        ],
        compiler_params=pltpu.CompilerParams(vmem_limit_bytes=56 * 2**20),
    )(*results)


def solution(mesh):
    nl, nz, no = mesh.shape["lsec"], mesh.shape["rsec"], mesh.shape["ops"]

    def on_device(psi, left_ops, right_ops, *tables):
        gathered = no * nl * nz * left_ops.size * left_ops.dtype.itemsize
        if no == 2 and nl == 4 and nz > 2 and left_ops.shape[0] > 1 and 3 * gathered <= VMEM_BUDGET:
            return by_kernel(nz, nl, psi, left_ops, right_ops, *tables)
        return by_collectives(psi, left_ops, right_ops, *tables)

    placed = (
        P(("lsec", "rsec"), None, None, None),
        P("ops", ("lsec", "rsec"), None, None),
        P("ops", ("lsec", "rsec"), None, None),
        P(),
        P(),
        P(),
        P(),
        P(),
        P(),
    )
    return jax.shard_map(
        on_device,
        mesh=mesh,
        in_specs=placed,
        out_specs=(P(("lsec", "rsec"), None, None, None), P(("lsec", "rsec"), "ops", None, None)),
        check_vma=False,
    )
```

```python
import functools

import jax
import jax.numpy as jnp
from jax import lax
from jax.experimental import pallas as pl
from jax.experimental.pallas import tpu as pltpu
from jax.sharding import PartitionSpec as P

SPREAD = 1
VMEM_BUDGET = 24 * 2**20
MESH = pl.DeviceIdType.MESH


def relayout(blocks):
    return lax.all_to_all(blocks, ("lsec", "rsec"), split_axis=1, concat_axis=1, tiled=True)


def inverse(order):
    count = order.shape[0]
    return jnp.zeros((count,), jnp.int32).at[order].set(jnp.arange(count, dtype=jnp.int32))


def by_collectives(
    psi, left_ops, right_ops, left_order, right_order, left_qn, right_qn, left_dims, right_dims
):
    slot = lax.axis_index(("lsec", "rsec"))
    width = psi.shape[-1]
    line = jnp.arange(width, dtype=jnp.int32)
    left_sector = left_order[slot]
    right_sector = right_order[slot]
    inv_left = inverse(left_order)
    inv_right = inverse(right_order)
    left_here = left_ops[:, 0]
    right_here = right_ops[:, 0]
    allowed_row = jnp.abs(left_qn[left_sector] - right_qn) <= SPREAD
    row_used = line < left_dims[left_sector]
    col_used = line[None, :] < right_dims[:, None]
    mask_left = allowed_row[:, None, None] & row_used[None, :, None] & col_used[:, None, :]
    allowed_col = jnp.abs(left_qn - right_qn[right_sector]) <= SPREAD
    rows_used = line[None, :] < left_dims[:, None]
    cols_here = line < right_dims[right_sector]
    mask_right = allowed_col[:, None, None] & rows_used[:, :, None] & cols_here[None, None, :]
    start = jnp.where(mask_left, psi[0], jnp.zeros((), jnp.bfloat16))
    start_slots = start[right_order]
    lefted = jnp.einsum(
        "kxy,byz->kbxz", left_here, start_slots, preferred_element_type=jnp.float32
    ).astype(jnp.bfloat16)
    arrived = relayout(lefted)
    partial_value = jnp.einsum(
        "kixy,kzy->ixz", arrived, right_here, preferred_element_type=jnp.float32
    )
    partial_value = partial_value[inv_left]
    summed = lax.psum(partial_value.astype(jnp.bfloat16), "ops").astype(jnp.float32)
    first = jnp.where(mask_right, summed, 0.0).astype(jnp.bfloat16)
    first_slots = first[left_order]
    righted = jnp.einsum(
        "ixy,kzy->kixz", first_slots, right_here, preferred_element_type=jnp.float32
    ).astype(jnp.bfloat16)
    returned = relayout(righted)
    second_partial = jnp.einsum(
        "kxy,kjyz->jxz", left_here, returned, preferred_element_type=jnp.float32
    )
    second_partial = second_partial[inv_right]
    second_share = lax.psum_scatter(
        second_partial.astype(jnp.bfloat16), "ops", scatter_dimension=0, tiled=True
    ).astype(jnp.float32)
    count = second_share.shape[0]
    mask_second = lax.dynamic_slice_in_dim(mask_left, lax.axis_index("ops") * count, count, 0)
    second = jnp.where(mask_second, second_share, 0.0).astype(jnp.bfloat16)
    return (first[None], second[None])


def kernel(
    nz,
    nl,
    psi_hbm,
    left_hbm,
    right_hbm,
    left_order_hbm,
    right_order_hbm,
    left_qn_hbm,
    right_qn_hbm,
    left_dims_hbm,
    right_dims_hbm,
    first_ref,
    second_ref,
    psi,
    left_order,
    right_order,
    left_qn,
    right_qn,
    left_dims,
    right_dims,
    right_own,
    lsem,
    rbuf,
    lbuf,
    start,
    terms,
    sigma,
    landed,
    lsend,
    lrecv,
    zsend,
    zrecv,
    xsend,
    xrecv,
    ysend,
    yrecv,
    dsend,
    drecv,
    csend,
    crecv,
    ssend,
    srecv,
    fsend,
    frecv,
    first,
    second,
    inverse_left,
    osem,
):
    l = lax.axis_index("lsec")
    z = lax.axis_index("rsec")
    o = lax.axis_index("ops")
    xp = (l + 2) % nl
    cp = l + 1 - 2 * (l % 2)
    op = 1 - o
    me = l * nz + z
    slots = nl * nz
    width = psi.shape[-1]
    kdev = lbuf.shape[1]
    to_y = {"ops": op}
    to_x = {"lsec": xp}
    to_c = {"lsec": cp}
    sent = []

    def send(src, dst, send_sem, recv_sem, where):
        copy = pltpu.make_async_remote_copy(
            src_ref=src,
            dst_ref=dst,
            send_sem=send_sem,
            recv_sem=recv_sem,
            device_id=where,
            device_id_type=MESH,
        )
        copy.start()
        sent.append(copy)

    def arrive(ref, sem):
        pltpu.make_async_copy(ref, ref, sem).wait()

    loads = [
        pltpu.make_async_copy(src, dst, lsem.at[i])
        for i, (src, dst) in enumerate(
            (
                (right_hbm.at[:, 0], right_own),
                (left_hbm.at[:, 0], lbuf.at[o]),
                (left_order_hbm, left_order),
                (right_order_hbm, right_order),
                (left_qn_hbm, left_qn),
                (right_qn_hbm, right_qn),
                (left_dims_hbm, left_dims),
                (right_dims_hbm, right_dims),
                (psi_hbm.at[0], psi),
            )
        )
    ]
    for load in loads:
        load.start()

    barrier = pltpu.get_barrier_semaphore()
    for s in range(nz):
        for t in range(nl):
            if s or t:
                pl.semaphore_signal(
                    barrier,
                    inc=1,
                    device_id={"lsec": (l + t) % nl, "rsec": (z + s) % nz},
                    device_id_type=MESH,
                )
    pl.semaphore_signal(barrier, inc=1, device_id=to_y, device_id_type=MESH)
    loads[0].wait()
    for k in range(kdev):
        rbuf[me, o, k] = right_own[k].astype(jnp.float32).T.astype(jnp.bfloat16)
    pl.semaphore_wait(barrier, slots)

    pair = z + 1 - 2 * (z % 2)
    group = [z, pair, (z + 2) % nz, (pair + 2) % nz]

    def slot_of(lane, s):
        return lane * nz + group[s]

    def stage_one(s):
        piece = rbuf.at[slot_of(l, s), o]
        if s:
            arrive(piece, zrecv.at[s])
        if s == 2:
            send(piece, piece, zsend.at[3], zrecv.at[3], {"rsec": pair})
        send(piece, piece, ysend.at[s], yrecv.at[s], to_y)
        send(piece, piece, xsend.at[s], xrecv.at[s], to_x)

    def stage_two(s):
        mine, theirs = slot_of(l, s), slot_of(xp, s)
        arrive(rbuf.at[theirs, o], xrecv.at[s])
        cut = 0 if s == 1 else 1
        if cut:
            half = rbuf.at[theirs, o, 0]
            send(half, half, dsend.at[0, s], drecv.at[0, s], to_y)
        arrive(rbuf.at[mine, op], yrecv.at[s])
        rest = rbuf.at[mine, op, pl.ds(cut, kdev - cut)]
        send(rest, rest, dsend.at[1, s], drecv.at[1, s], to_x)
        send(rbuf.at[mine], rbuf.at[mine], csend.at[0, s], crecv.at[0, s], to_c)

    def stage_three(s):
        theirs = slot_of(xp, s)
        cut = 0 if s == 1 else 1
        if cut:
            arrive(rbuf.at[theirs, op, 0], drecv.at[0, s])
        arrive(rbuf.at[theirs, op, pl.ds(cut, kdev - cut)], drecv.at[1, s])
        send(rbuf.at[theirs], rbuf.at[theirs], csend.at[1, s], crecv.at[1, s], to_c)

    def stage_four(s):
        arrive(rbuf.at[slot_of(cp, s)], crecv.at[0, s])
        arrive(rbuf.at[slot_of((cp + 2) % nl, s)], crecv.at[1, s])

    for s in (1, 2):
        piece = rbuf.at[me, o]
        send(piece, piece, zsend.at[s], zrecv.at[s], {"rsec": group[s]})
    stage_one(0)
    loads[1].wait()
    send(lbuf.at[o], lbuf.at[o], lsend, lrecv, to_y)
    for load in loads[2:]:
        load.wait()

    sector = left_order[me]
    my_qn = left_qn[sector]
    rows = lax.broadcasted_iota(jnp.int32, (width, width), 0)
    cols = lax.broadcasted_iota(jnp.int32, (width, width), 1)
    rows_used = rows < left_dims[sector]

    def masked(value, b):
        used = jnp.where(jnp.abs(my_qn - right_qn[b]) <= SPREAD, right_dims[b], 0)
        return jnp.where(rows_used & (cols < used), value, 0.0).astype(jnp.bfloat16)

    def start_pair(pair, carry):
        blocks = []
        for j in (2 * pair, 2 * pair + 1):
            b = right_order[j]
            blocks.append(masked(psi[b].astype(jnp.float32), b))
        start[pair] = jnp.concatenate(blocks, axis=1)
        return carry

    def terms_pair(pair, carry):
        for h in range(2):
            both = jnp.dot(
                lbuf[h].reshape(kdev * width, width),
                start[pair],
                preferred_element_type=jnp.float32,
            )
            both = both.astype(jnp.bfloat16).reshape(kdev, width, 2 * width)
            terms[2 * pair, h] = both[:, :, :width]
            terms[2 * pair + 1, h] = both[:, :, width:]
        return carry

    def lanes(ref, j):
        return jnp.concatenate([ref[j, h, k] for h in range(2) for k in range(kdev)], axis=1)

    def first_value(j, b):
        value = jnp.dot(
            lanes(terms, j),
            rbuf[j].reshape(2 * kdev * width, width),
            preferred_element_type=jnp.float32,
        )
        return masked(value, b)

    def first_block(j):
        sigma[j] = first_value(j, right_order[j])

    def direct(plane, s):
        if s == 0:
            return list(range(1, nl))
        return [2 * u + (plane + s) % 2 for u in range(nl // 2)]

    def source_of(s, t):
        return ((l + nl - t) % nl) * nz + group[s]

    def first_direct(s):
        targets = [(l + t) % nl for t in direct(o, s)]
        for there in targets:
            first_block(slot_of(there, s))
        for u, there in enumerate(targets):
            send(
                sigma.at[slot_of(there, s)],
                landed.at[me],
                ssend.at[s, u],
                srecv.at[s, u],
                {"lsec": there, "rsec": group[s]},
            )

    def relay(s):
        for u in range(nl // 2):
            block = landed.at[source_of(s, direct(o, s)[u])]
            arrive(block, srecv.at[s, u])
            send(block, block, fsend.at[s, u], frecv.at[s, u], to_y)

    lax.fori_loop(0, slots // 2, start_pair, 0, unroll=2)
    stage_one(1)
    stage_two(0)
    arrive(lbuf.at[op], lrecv)
    def slot_holding(order, wanted):
        found = jnp.int32(0)
        for j in range(slots):
            found = jnp.where(order[j] == wanted, j, found)
        return found

    def find(a, carry):
        inverse_left[a] = slot_holding(left_order, a)
        return carry

    lax.fori_loop(0, slots, find, 0)
    quarter = slots // 4
    lax.fori_loop(0, quarter, terms_pair, 0, unroll=2)
    for step in range(2, nz + 3):
        if step < nz:
            stage_one(step)
        if 1 <= step - 1 < nz:
            stage_two(step - 1)
        if 0 <= step - 2 < nz:
            stage_three(step - 2)
        if step == 2:
            lax.fori_loop(quarter, 2 * quarter, terms_pair, 0, unroll=2)
        if 0 <= step - 3 < nz:
            stage_four(step - 3)
            first_direct(step - 3)
        if 0 < step - 5 < nz - 2:
            relay(step - 5)

    first_block(me)
    landed[me] = sigma[me]
    relay(nz - 2)

    count = second_ref.shape[1]
    left_wide = jnp.concatenate([lbuf[h, k] for h in range(2) for k in range(kdev)], axis=1)

    def second_pair(i, carry):
        inner = []
        for n in range(2):
            b = o * count + 2 * i + n
            j = slot_holding(right_order, b)
            state = first_value(j, b)
            part = jnp.dot(state, lanes(rbuf, j), preferred_element_type=jnp.float32)
            part = part.astype(jnp.bfloat16)
            halves = [part[:, k * width : (k + 1) * width] for k in range(2 * kdev)]
            inner.append(jnp.concatenate(halves, axis=0))
        both = jnp.dot(
            left_wide, jnp.concatenate(inner, axis=1), preferred_element_type=jnp.float32
        )
        for n in range(2):
            second[2 * i + n] = masked(
                both[:, n * width : (n + 1) * width], o * count + 2 * i + n
            )
        return carry

    lax.fori_loop(0, count // 4, second_pair, 0)
    relay(nz - 1)
    lax.fori_loop(count // 4, count // 2, second_pair, 0)
    out_second = pltpu.make_async_copy(second, second_ref.at[0], osem.at[0])
    out_second.start()

    for u, t in enumerate(direct(o, 0)):
        arrive(landed.at[source_of(0, t)], srecv.at[0, u])
    for s in range(1, nz):
        for u in range(nl // 2):
            arrive(landed.at[source_of(s, direct(op, s)[u])], frecv.at[s, u])

    def place(a, carry):
        first[a] = landed[inverse_left[a]]
        return carry

    lax.fori_loop(0, slots, place, 0, unroll=4)
    out_first = pltpu.make_async_copy(first, first_ref.at[0], osem.at[1])
    out_first.start()
    for copy in sent:
        copy.wait_send()
    out_second.wait()
    out_first.wait()


def hand_over(parts, first_in, second_in, first_out, second_out, first, second, sem):
    ins, outs = [], []
    for n, (src, mid, dst) in enumerate(
        ((second_in, second, second_out), (first_in, first, first_out))
    ):
        size = mid.shape[0] // parts
        for i in range(parts):
            rows = pl.ds(i * size, size)
            ins.append(pltpu.make_async_copy(src.at[0, rows], mid.at[rows], sem.at[0, n, i]))
            outs.append(pltpu.make_async_copy(mid.at[rows], dst.at[0, rows], sem.at[1, n, i]))
    for copy in ins:
        copy.start()
    for arrived, copy in zip(ins, outs):
        arrived.wait()
        copy.start()
    for copy in outs:
        copy.wait()


def by_kernel(nz, nl, psi, left_ops, right_ops, *tables):
    slots = nl * nz
    width = psi.shape[-1]
    kdev = left_ops.shape[0]
    block = (width, width)
    dma = pltpu.SemaphoreType.DMA
    bf16 = jnp.bfloat16
    hbm = pl.BlockSpec(memory_space=pltpu.HBM)
    flops = 2 * width**3 * 2 * kdev * slots * 3
    shapes = (
        jax.ShapeDtypeStruct((1, slots) + block, bf16),
        jax.ShapeDtypeStruct((1, slots // 2) + block, bf16),
    )
    results = pl.pallas_call(
        functools.partial(kernel, nz, nl),
        out_shape=shapes,
        in_specs=[hbm] * 9,
        out_specs=(hbm, hbm),
        scratch_shapes=[
            pltpu.VMEM((slots,) + block, bf16),
            *[pltpu.SMEM(table.shape, jnp.int32) for table in tables],
            pltpu.VMEM((kdev,) + block, bf16),
            dma((9,)),
            pltpu.VMEM((slots, 2, kdev) + block, bf16),
            pltpu.VMEM((2, kdev) + block, bf16),
            pltpu.VMEM((slots // 2, width, 2 * width), bf16),
            pltpu.VMEM((slots, 2, kdev) + block, bf16),
            pltpu.VMEM((slots,) + block, bf16),
            pltpu.VMEM((slots,) + block, bf16),
            dma,
            dma,
            dma((nz,)),
            dma((nz,)),
            dma((nz,)),
            dma((nz,)),
            dma((nz,)),
            dma((nz,)),
            dma((2, nz)),
            dma((2, nz)),
            dma((2, nz)),
            dma((2, nz)),
            dma((nz, nl)),
            dma((nz, nl)),
            dma((nz, nl // 2)),
            dma((nz, nl // 2)),
            pltpu.VMEM((slots,) + block, bf16),
            pltpu.VMEM((slots // 2,) + block, bf16),
            pltpu.SMEM((slots,), jnp.int32),
            dma((2,)),
        ],
        compiler_params=pltpu.CompilerParams(
            collective_id=0, has_side_effects=True, vmem_limit_bytes=56 * 2**20
        ),
        cost_estimate=pl.CostEstimate(flops=flops, bytes_accessed=4 * 2**20, transcendentals=0),
    )(psi, left_ops, right_ops, *tables)
    parts = 4
    return pl.pallas_call(
        functools.partial(hand_over, parts),
        out_shape=shapes,
        in_specs=[hbm] * 2,
        out_specs=(hbm, hbm),
        scratch_shapes=[
            pltpu.VMEM((slots,) + block, bf16),
            pltpu.VMEM((slots // 2,) + block, bf16),
            dma((2, 2, parts)),
        ],
        compiler_params=pltpu.CompilerParams(vmem_limit_bytes=56 * 2**20),
    )(*results)


def solution(mesh):
    nl, nz, no = mesh.shape["lsec"], mesh.shape["rsec"], mesh.shape["ops"]

    def on_device(psi, left_ops, right_ops, *tables):
        gathered = no * nl * nz * left_ops.size * left_ops.dtype.itemsize
        if no == 2 and nl == 4 and nz == 4 and left_ops.shape[0] > 1 and 3 * gathered <= VMEM_BUDGET:
            return by_kernel(nz, nl, psi, left_ops, right_ops, *tables)
        return by_collectives(psi, left_ops, right_ops, *tables)

    placed = (
        P(("lsec", "rsec"), None, None, None),
        P("ops", ("lsec", "rsec"), None, None),
        P("ops", ("lsec", "rsec"), None, None),
        P(),
        P(),
        P(),
        P(),
        P(),
        P(),
    )
    return jax.shard_map(
        on_device,
        mesh=mesh,
        in_specs=placed,
        out_specs=(P(("lsec", "rsec"), None, None, None), P(("lsec", "rsec"), "ops", None, None)),
        check_vma=False,
    )
```

```python
import functools

import jax
import jax.numpy as jnp
from jax import lax
from jax.experimental import pallas as pl
from jax.experimental.pallas import tpu as pltpu
from jax.sharding import PartitionSpec as P

SPREAD = 1
VMEM_BUDGET = 24 * 2**20
MESH = pl.DeviceIdType.MESH


def relayout(blocks):
    return lax.all_to_all(blocks, ("lsec", "rsec"), split_axis=1, concat_axis=1, tiled=True)


def inverse(order):
    count = order.shape[0]
    return jnp.zeros((count,), jnp.int32).at[order].set(jnp.arange(count, dtype=jnp.int32))


def by_collectives(
    psi, left_ops, right_ops, left_order, right_order, left_qn, right_qn, left_dims, right_dims
):
    slot = lax.axis_index(("lsec", "rsec"))
    width = psi.shape[-1]
    line = jnp.arange(width, dtype=jnp.int32)
    left_sector = left_order[slot]
    right_sector = right_order[slot]
    inv_left = inverse(left_order)
    inv_right = inverse(right_order)
    left_here = left_ops[:, 0]
    right_here = right_ops[:, 0]
    allowed_row = jnp.abs(left_qn[left_sector] - right_qn) <= SPREAD
    row_used = line < left_dims[left_sector]
    col_used = line[None, :] < right_dims[:, None]
    mask_left = allowed_row[:, None, None] & row_used[None, :, None] & col_used[:, None, :]
    allowed_col = jnp.abs(left_qn - right_qn[right_sector]) <= SPREAD
    rows_used = line[None, :] < left_dims[:, None]
    cols_here = line < right_dims[right_sector]
    mask_right = allowed_col[:, None, None] & rows_used[:, :, None] & cols_here[None, None, :]
    start = jnp.where(mask_left, psi[0], jnp.zeros((), jnp.bfloat16))
    start_slots = start[right_order]
    lefted = jnp.einsum(
        "kxy,byz->kbxz", left_here, start_slots, preferred_element_type=jnp.float32
    ).astype(jnp.bfloat16)
    arrived = relayout(lefted)
    partial_value = jnp.einsum(
        "kixy,kzy->ixz", arrived, right_here, preferred_element_type=jnp.float32
    )
    partial_value = partial_value[inv_left]
    summed = lax.psum(partial_value.astype(jnp.bfloat16), "ops").astype(jnp.float32)
    first = jnp.where(mask_right, summed, 0.0).astype(jnp.bfloat16)
    first_slots = first[left_order]
    righted = jnp.einsum(
        "ixy,kzy->kixz", first_slots, right_here, preferred_element_type=jnp.float32
    ).astype(jnp.bfloat16)
    returned = relayout(righted)
    second_partial = jnp.einsum(
        "kxy,kjyz->jxz", left_here, returned, preferred_element_type=jnp.float32
    )
    second_partial = second_partial[inv_right]
    second_share = lax.psum_scatter(
        second_partial.astype(jnp.bfloat16), "ops", scatter_dimension=0, tiled=True
    ).astype(jnp.float32)
    count = second_share.shape[0]
    mask_second = lax.dynamic_slice_in_dim(mask_left, lax.axis_index("ops") * count, count, 0)
    second = jnp.where(mask_second, second_share, 0.0).astype(jnp.bfloat16)
    return (first[None], second[None])


def kernel(
    nz,
    nl,
    psi_hbm,
    left_hbm,
    right_hbm,
    left_order_hbm,
    right_order_hbm,
    left_qn_hbm,
    right_qn_hbm,
    left_dims_hbm,
    right_dims_hbm,
    first_ref,
    second_ref,
    psi,
    left_order,
    right_order,
    left_qn,
    right_qn,
    left_dims,
    right_dims,
    right_own,
    lsem,
    rbuf,
    lbuf,
    start,
    terms,
    sigma,
    landed,
    lsend,
    lrecv,
    zsend,
    zrecv,
    xsend,
    xrecv,
    ysend,
    yrecv,
    dsend,
    drecv,
    csend,
    crecv,
    ssend,
    srecv,
    fsend,
    frecv,
    first,
    second,
    inverse_left,
    osem,
):
    l = lax.axis_index("lsec")
    z = lax.axis_index("rsec")
    o = lax.axis_index("ops")
    xp = (l + 2) % nl
    cp = l + 1 - 2 * (l % 2)
    op = 1 - o
    me = l * nz + z
    slots = nl * nz
    width = psi.shape[-1]
    kdev = lbuf.shape[1]
    to_y = {"ops": op}
    to_x = {"lsec": xp}
    to_c = {"lsec": cp}
    sent = []

    def send(src, dst, send_sem, recv_sem, where):
        copy = pltpu.make_async_remote_copy(
            src_ref=src,
            dst_ref=dst,
            send_sem=send_sem,
            recv_sem=recv_sem,
            device_id=where,
            device_id_type=MESH,
        )
        copy.start()
        sent.append(copy)

    def arrive(ref, sem):
        pltpu.make_async_copy(ref, ref, sem).wait()

    loads = [
        pltpu.make_async_copy(src, dst, lsem.at[i])
        for i, (src, dst) in enumerate(
            (
                (right_hbm.at[:, 0], right_own),
                (left_hbm.at[:, 0], lbuf.at[o]),
                (left_order_hbm, left_order),
                (right_order_hbm, right_order),
                (left_qn_hbm, left_qn),
                (right_qn_hbm, right_qn),
                (left_dims_hbm, left_dims),
                (right_dims_hbm, right_dims),
                (psi_hbm.at[0], psi),
            )
        )
    ]
    for load in loads:
        load.start()

    barrier = pltpu.get_barrier_semaphore()
    for s in range(nz):
        for t in range(nl):
            if s or t:
                pl.semaphore_signal(
                    barrier,
                    inc=1,
                    device_id={"lsec": (l + t) % nl, "rsec": (z + s) % nz},
                    device_id_type=MESH,
                )
    pl.semaphore_signal(barrier, inc=1, device_id=to_y, device_id_type=MESH)
    loads[0].wait()
    for k in range(kdev):
        rbuf[me, o, k] = right_own[k].astype(jnp.float32).T.astype(jnp.bfloat16)
    pl.semaphore_wait(barrier, slots)

    pair = z + 1 - 2 * (z % 2)
    group = [z, pair, (z + 2) % nz, (pair + 2) % nz]

    def slot_of(lane, s):
        return lane * nz + group[s]

    def stage_one(s):
        piece = rbuf.at[slot_of(l, s), o]
        if s:
            arrive(piece, zrecv.at[s])
        if s == 2:
            send(piece, piece, zsend.at[3], zrecv.at[3], {"rsec": pair})
        send(piece, piece, ysend.at[s], yrecv.at[s], to_y)
        send(piece, piece, xsend.at[s], xrecv.at[s], to_x)

    def stage_two(s):
        mine, theirs = slot_of(l, s), slot_of(xp, s)
        arrive(rbuf.at[theirs, o], xrecv.at[s])
        cut = 0 if s == 1 else 1
        if cut:
            half = rbuf.at[theirs, o, 0]
            send(half, half, dsend.at[0, s], drecv.at[0, s], to_y)
        arrive(rbuf.at[mine, op], yrecv.at[s])
        rest = rbuf.at[mine, op, pl.ds(cut, kdev - cut)]
        send(rest, rest, dsend.at[1, s], drecv.at[1, s], to_x)
        send(rbuf.at[mine], rbuf.at[mine], csend.at[0, s], crecv.at[0, s], to_c)

    def stage_three(s):
        theirs = slot_of(xp, s)
        cut = 0 if s == 1 else 1
        if cut:
            arrive(rbuf.at[theirs, op, 0], drecv.at[0, s])
        arrive(rbuf.at[theirs, op, pl.ds(cut, kdev - cut)], drecv.at[1, s])
        send(rbuf.at[theirs], rbuf.at[theirs], csend.at[1, s], crecv.at[1, s], to_c)

    def stage_four(s):
        arrive(rbuf.at[slot_of(cp, s)], crecv.at[0, s])
        arrive(rbuf.at[slot_of((cp + 2) % nl, s)], crecv.at[1, s])

    for s in (1, 2):
        piece = rbuf.at[me, o]
        send(piece, piece, zsend.at[s], zrecv.at[s], {"rsec": group[s]})
    stage_one(0)
    loads[1].wait()
    send(lbuf.at[o], lbuf.at[o], lsend, lrecv, to_y)
    for load in loads[2:]:
        load.wait()

    sector = left_order[me]
    my_qn = left_qn[sector]
    rows = lax.broadcasted_iota(jnp.int32, (width, width), 0)
    cols = lax.broadcasted_iota(jnp.int32, (width, width), 1)
    rows_used = rows < left_dims[sector]

    def masked(value, b):
        used = jnp.where(jnp.abs(my_qn - right_qn[b]) <= SPREAD, right_dims[b], 0)
        return jnp.where(rows_used & (cols < used), value, 0.0).astype(jnp.bfloat16)

    def left_terms(h, two):
        both = jnp.dot(
            lbuf[h].reshape(kdev * width, width), start[two], preferred_element_type=jnp.float32
        )
        both = both.astype(jnp.bfloat16).reshape(kdev, width, 2 * width)
        terms[2 * two, h] = both[:, :, :width]
        terms[2 * two + 1, h] = both[:, :, width:]

    def own_terms(two, carry):
        blocks = []
        for j in (2 * two, 2 * two + 1):
            b = right_order[j]
            blocks.append(masked(psi[b].astype(jnp.float32), b))
        start[two] = jnp.concatenate(blocks, axis=1)
        left_terms(o, two)
        return carry

    def other_terms(two, carry):
        left_terms(op, two)
        return carry

    def lanes(ref, j):
        return jnp.concatenate([ref[j, h, k] for h in range(2) for k in range(kdev)], axis=1)

    def first_value(j, b):
        value = jnp.dot(
            lanes(terms, j),
            rbuf[j].reshape(2 * kdev * width, width),
            preferred_element_type=jnp.float32,
        )
        return masked(value, b)

    def first_block(j):
        sigma[j] = first_value(j, right_order[j])

    def direct(plane, s):
        if s == 0:
            return list(range(1, nl))
        return [2 * u + (plane + s) % 2 for u in range(nl // 2)]

    def source_of(s, t):
        return ((l + nl - t) % nl) * nz + group[s]

    def first_direct(s):
        targets = [(l + t) % nl for t in direct(o, s)]
        for there in targets:
            first_block(slot_of(there, s))
        for u, there in enumerate(targets):
            send(
                sigma.at[slot_of(there, s)],
                landed.at[me],
                ssend.at[s, u],
                srecv.at[s, u],
                {"lsec": there, "rsec": group[s]},
            )

    def relay(s):
        for u in range(nl // 2):
            block = landed.at[source_of(s, direct(o, s)[u])]
            arrive(block, srecv.at[s, u])
            send(block, block, fsend.at[s, u], frecv.at[s, u], to_y)

    lax.fori_loop(0, slots // 2, own_terms, 0, unroll=2)
    stage_one(1)
    stage_two(0)
    def slot_holding(order, wanted):
        found = jnp.int32(0)
        for j in range(slots):
            found = jnp.where(order[j] == wanted, j, found)
        return found

    def find(a, carry):
        inverse_left[a] = slot_holding(left_order, a)
        return carry

    for step in range(2, nz + 3):
        if step < nz:
            stage_one(step)
        if 1 <= step - 1 < nz:
            stage_two(step - 1)
        if 0 <= step - 2 < nz:
            stage_three(step - 2)
        if step == 2:
            arrive(lbuf.at[op], lrecv)
            lax.fori_loop(0, slots // 2, other_terms, 0, unroll=2)
            lax.fori_loop(0, slots, find, 0)
        if 0 <= step - 3 < nz:
            stage_four(step - 3)
            first_direct(step - 3)
        if 0 < step - 5 < nz - 2:
            relay(step - 5)

    first_block(me)
    landed[me] = sigma[me]
    relay(nz - 2)

    count = second_ref.shape[1]
    left_wide = jnp.concatenate([lbuf[h, k] for h in range(2) for k in range(kdev)], axis=1)

    def second_pair(i, carry):
        inner = []
        for n in range(2):
            b = o * count + 2 * i + n
            j = slot_holding(right_order, b)
            state = first_value(j, b)
            part = jnp.dot(state, lanes(rbuf, j), preferred_element_type=jnp.float32)
            part = part.astype(jnp.bfloat16)
            halves = [part[:, k * width : (k + 1) * width] for k in range(2 * kdev)]
            inner.append(jnp.concatenate(halves, axis=0))
        both = jnp.dot(
            left_wide, jnp.concatenate(inner, axis=1), preferred_element_type=jnp.float32
        )
        for n in range(2):
            second[2 * i + n] = masked(
                both[:, n * width : (n + 1) * width], o * count + 2 * i + n
            )
        return carry

    lax.fori_loop(0, count // 4, second_pair, 0)
    relay(nz - 1)
    lax.fori_loop(count // 4, count // 2, second_pair, 0)
    out_second = pltpu.make_async_copy(second, second_ref.at[0], osem.at[0])
    out_second.start()

    for u, t in enumerate(direct(o, 0)):
        arrive(landed.at[source_of(0, t)], srecv.at[0, u])
    for s in range(1, nz):
        for u in range(nl // 2):
            arrive(landed.at[source_of(s, direct(op, s)[u])], frecv.at[s, u])

    def place(a, carry):
        first[a] = landed[inverse_left[a]]
        return carry

    lax.fori_loop(0, slots, place, 0, unroll=4)
    out_first = pltpu.make_async_copy(first, first_ref.at[0], osem.at[1])
    out_first.start()
    for copy in sent:
        copy.wait_send()
    out_second.wait()
    out_first.wait()


def hand_over(parts, first_in, second_in, first_out, second_out, first, second, sem):
    ins, outs = [], []
    for n, (src, mid, dst) in enumerate(
        ((second_in, second, second_out), (first_in, first, first_out))
    ):
        size = mid.shape[0] // parts
        for i in range(parts):
            rows = pl.ds(i * size, size)
            ins.append(pltpu.make_async_copy(src.at[0, rows], mid.at[rows], sem.at[0, n, i]))
            outs.append(pltpu.make_async_copy(mid.at[rows], dst.at[0, rows], sem.at[1, n, i]))
    for copy in ins:
        copy.start()
    for arrived, copy in zip(ins, outs):
        arrived.wait()
        copy.start()
    for copy in outs:
        copy.wait()


def by_kernel(nz, nl, psi, left_ops, right_ops, *tables):
    slots = nl * nz
    width = psi.shape[-1]
    kdev = left_ops.shape[0]
    block = (width, width)
    dma = pltpu.SemaphoreType.DMA
    bf16 = jnp.bfloat16
    hbm = pl.BlockSpec(memory_space=pltpu.HBM)
    flops = 2 * width**3 * 2 * kdev * slots * 3
    shapes = (
        jax.ShapeDtypeStruct((1, slots) + block, bf16),
        jax.ShapeDtypeStruct((1, slots // 2) + block, bf16),
    )
    results = pl.pallas_call(
        functools.partial(kernel, nz, nl),
        out_shape=shapes,
        in_specs=[hbm] * 9,
        out_specs=(hbm, hbm),
        scratch_shapes=[
            pltpu.VMEM((slots,) + block, bf16),
            *[pltpu.SMEM(table.shape, jnp.int32) for table in tables],
            pltpu.VMEM((kdev,) + block, bf16),
            dma((9,)),
            pltpu.VMEM((slots, 2, kdev) + block, bf16),
            pltpu.VMEM((2, kdev) + block, bf16),
            pltpu.VMEM((slots // 2, width, 2 * width), bf16),
            pltpu.VMEM((slots, 2, kdev) + block, bf16),
            pltpu.VMEM((slots,) + block, bf16),
            pltpu.VMEM((slots,) + block, bf16),
            dma,
            dma,
            dma((nz,)),
            dma((nz,)),
            dma((nz,)),
            dma((nz,)),
            dma((nz,)),
            dma((nz,)),
            dma((2, nz)),
            dma((2, nz)),
            dma((2, nz)),
            dma((2, nz)),
            dma((nz, nl)),
            dma((nz, nl)),
            dma((nz, nl // 2)),
            dma((nz, nl // 2)),
            pltpu.VMEM((slots,) + block, bf16),
            pltpu.VMEM((slots // 2,) + block, bf16),
            pltpu.SMEM((slots,), jnp.int32),
            dma((2,)),
        ],
        compiler_params=pltpu.CompilerParams(
            collective_id=0, has_side_effects=True, vmem_limit_bytes=56 * 2**20
        ),
        cost_estimate=pl.CostEstimate(flops=flops, bytes_accessed=4 * 2**20, transcendentals=0),
    )(psi, left_ops, right_ops, *tables)
    parts = 4
    return pl.pallas_call(
        functools.partial(hand_over, parts),
        out_shape=shapes,
        in_specs=[hbm] * 2,
        out_specs=(hbm, hbm),
        scratch_shapes=[
            pltpu.VMEM((slots,) + block, bf16),
            pltpu.VMEM((slots // 2,) + block, bf16),
            dma((2, 2, parts)),
        ],
        compiler_params=pltpu.CompilerParams(vmem_limit_bytes=56 * 2**20),
    )(*results)


def solution(mesh):
    nl, nz, no = mesh.shape["lsec"], mesh.shape["rsec"], mesh.shape["ops"]

    def on_device(psi, left_ops, right_ops, *tables):
        gathered = no * nl * nz * left_ops.size * left_ops.dtype.itemsize
        if no == 2 and nl == 4 and nz == 4 and left_ops.shape[0] > 1 and 3 * gathered <= VMEM_BUDGET:
            return by_kernel(nz, nl, psi, left_ops, right_ops, *tables)
        return by_collectives(psi, left_ops, right_ops, *tables)

    placed = (
        P(("lsec", "rsec"), None, None, None),
        P("ops", ("lsec", "rsec"), None, None),
        P("ops", ("lsec", "rsec"), None, None),
        P(),
        P(),
        P(),
        P(),
        P(),
        P(),
    )
    return jax.shard_map(
        on_device,
        mesh=mesh,
        in_specs=placed,
        out_specs=(P(("lsec", "rsec"), None, None, None), P(("lsec", "rsec"), "ops", None, None)),
        check_vma=False,
    )
```

```python
import functools

import jax
import jax.numpy as jnp
from jax import lax
from jax.experimental import pallas as pl
from jax.experimental.pallas import tpu as pltpu
from jax.sharding import PartitionSpec as P

SPREAD = 1
VMEM_BUDGET = 24 * 2**20
MESH = pl.DeviceIdType.MESH


def relayout(blocks):
    return lax.all_to_all(blocks, ("lsec", "rsec"), split_axis=1, concat_axis=1, tiled=True)


def inverse(order):
    count = order.shape[0]
    return jnp.zeros((count,), jnp.int32).at[order].set(jnp.arange(count, dtype=jnp.int32))


def by_collectives(
    psi, left_ops, right_ops, left_order, right_order, left_qn, right_qn, left_dims, right_dims
):
    slot = lax.axis_index(("lsec", "rsec"))
    width = psi.shape[-1]
    line = jnp.arange(width, dtype=jnp.int32)
    left_sector = left_order[slot]
    right_sector = right_order[slot]
    inv_left = inverse(left_order)
    inv_right = inverse(right_order)
    left_here = left_ops[:, 0]
    right_here = right_ops[:, 0]
    allowed_row = jnp.abs(left_qn[left_sector] - right_qn) <= SPREAD
    row_used = line < left_dims[left_sector]
    col_used = line[None, :] < right_dims[:, None]
    mask_left = allowed_row[:, None, None] & row_used[None, :, None] & col_used[:, None, :]
    allowed_col = jnp.abs(left_qn - right_qn[right_sector]) <= SPREAD
    rows_used = line[None, :] < left_dims[:, None]
    cols_here = line < right_dims[right_sector]
    mask_right = allowed_col[:, None, None] & rows_used[:, :, None] & cols_here[None, None, :]
    start = jnp.where(mask_left, psi[0], jnp.zeros((), jnp.bfloat16))
    start_slots = start[right_order]
    lefted = jnp.einsum(
        "kxy,byz->kbxz", left_here, start_slots, preferred_element_type=jnp.float32
    ).astype(jnp.bfloat16)
    arrived = relayout(lefted)
    partial_value = jnp.einsum(
        "kixy,kzy->ixz", arrived, right_here, preferred_element_type=jnp.float32
    )
    partial_value = partial_value[inv_left]
    summed = lax.psum(partial_value.astype(jnp.bfloat16), "ops").astype(jnp.float32)
    first = jnp.where(mask_right, summed, 0.0).astype(jnp.bfloat16)
    first_slots = first[left_order]
    righted = jnp.einsum(
        "ixy,kzy->kixz", first_slots, right_here, preferred_element_type=jnp.float32
    ).astype(jnp.bfloat16)
    returned = relayout(righted)
    second_partial = jnp.einsum(
        "kxy,kjyz->jxz", left_here, returned, preferred_element_type=jnp.float32
    )
    second_partial = second_partial[inv_right]
    second_share = lax.psum_scatter(
        second_partial.astype(jnp.bfloat16), "ops", scatter_dimension=0, tiled=True
    ).astype(jnp.float32)
    count = second_share.shape[0]
    mask_second = lax.dynamic_slice_in_dim(mask_left, lax.axis_index("ops") * count, count, 0)
    second = jnp.where(mask_second, second_share, 0.0).astype(jnp.bfloat16)
    return (first[None], second[None])


def kernel(
    nz,
    nl,
    psi_hbm,
    left_hbm,
    right_hbm,
    left_order_hbm,
    right_order_hbm,
    left_qn_hbm,
    right_qn_hbm,
    left_dims_hbm,
    right_dims_hbm,
    first_ref,
    second_ref,
    psi,
    left_order,
    right_order,
    left_qn,
    right_qn,
    left_dims,
    right_dims,
    right_own,
    lsem,
    rbuf,
    lbuf,
    start,
    terms,
    sigma,
    landed,
    lsend,
    lrecv,
    zsend,
    zrecv,
    xsend,
    xrecv,
    ysend,
    yrecv,
    dsend,
    drecv,
    csend,
    crecv,
    ssend,
    srecv,
    fsend,
    frecv,
    first,
    second,
    inverse_left,
    osem,
):
    l = lax.axis_index("lsec")
    z = lax.axis_index("rsec")
    o = lax.axis_index("ops")
    xp = (l + 2) % nl
    cp = l + 1 - 2 * (l % 2)
    op = 1 - o
    me = l * nz + z
    slots = nl * nz
    width = psi.shape[-1]
    kdev = lbuf.shape[1]
    to_y = {"ops": op}
    to_x = {"lsec": xp}
    to_c = {"lsec": cp}
    sent = []

    def send(src, dst, send_sem, recv_sem, where):
        copy = pltpu.make_async_remote_copy(
            src_ref=src,
            dst_ref=dst,
            send_sem=send_sem,
            recv_sem=recv_sem,
            device_id=where,
            device_id_type=MESH,
        )
        copy.start()
        sent.append(copy)

    def arrive(ref, sem):
        pltpu.make_async_copy(ref, ref, sem).wait()

    loads = [
        pltpu.make_async_copy(src, dst, lsem.at[i])
        for i, (src, dst) in enumerate(
            (
                (right_hbm.at[:, 0], right_own),
                (left_hbm.at[:, 0], lbuf.at[o]),
                (left_order_hbm, left_order),
                (right_order_hbm, right_order),
                (left_qn_hbm, left_qn),
                (right_qn_hbm, right_qn),
                (left_dims_hbm, left_dims),
                (right_dims_hbm, right_dims),
                (psi_hbm.at[0], psi),
            )
        )
    ]
    for load in loads:
        load.start()

    barrier = pltpu.get_barrier_semaphore()
    for s in range(nz):
        for t in range(nl):
            if s or t:
                pl.semaphore_signal(
                    barrier,
                    inc=1,
                    device_id={"lsec": (l + t) % nl, "rsec": (z + s) % nz},
                    device_id_type=MESH,
                )
    pl.semaphore_signal(barrier, inc=1, device_id=to_y, device_id_type=MESH)
    loads[0].wait()
    for k in range(kdev):
        rbuf[me, o, k] = right_own[k].astype(jnp.float32).T.astype(jnp.bfloat16)
    pl.semaphore_wait(barrier, slots)

    pair = z + 1 - 2 * (z % 2)
    group = [z, pair, (z + 2) % nz, (pair + 2) % nz]

    def slot_of(lane, s):
        return lane * nz + group[s]

    def stage_one(s):
        piece = rbuf.at[slot_of(l, s), o]
        if s:
            arrive(piece, zrecv.at[s])
        if s == 2:
            send(piece, piece, zsend.at[3], zrecv.at[3], {"rsec": pair})
        send(piece, piece, ysend.at[s], yrecv.at[s], to_y)
        send(piece, piece, xsend.at[s], xrecv.at[s], to_x)

    def stage_two(s):
        mine, theirs = slot_of(l, s), slot_of(xp, s)
        arrive(rbuf.at[theirs, o], xrecv.at[s])
        cut = 0 if s == 1 else 1
        if cut:
            half = rbuf.at[theirs, o, 0]
            send(half, half, dsend.at[0, s], drecv.at[0, s], to_y)
        arrive(rbuf.at[mine, op], yrecv.at[s])
        rest = rbuf.at[mine, op, pl.ds(cut, kdev - cut)]
        send(rest, rest, dsend.at[1, s], drecv.at[1, s], to_x)
        send(rbuf.at[mine], rbuf.at[mine], csend.at[0, s], crecv.at[0, s], to_c)

    def stage_three(s):
        theirs = slot_of(xp, s)
        cut = 0 if s == 1 else 1
        if cut:
            arrive(rbuf.at[theirs, op, 0], drecv.at[0, s])
        arrive(rbuf.at[theirs, op, pl.ds(cut, kdev - cut)], drecv.at[1, s])
        send(rbuf.at[theirs], rbuf.at[theirs], csend.at[1, s], crecv.at[1, s], to_c)

    def stage_four(s):
        arrive(rbuf.at[slot_of(cp, s)], crecv.at[0, s])
        arrive(rbuf.at[slot_of((cp + 2) % nl, s)], crecv.at[1, s])

    for s in (1, 2):
        piece = rbuf.at[me, o]
        send(piece, piece, zsend.at[s], zrecv.at[s], {"rsec": group[s]})
    stage_one(0)
    loads[1].wait()
    send(lbuf.at[o], lbuf.at[o], lsend, lrecv, to_y)
    for load in loads[2:]:
        load.wait()

    sector = left_order[me]
    my_qn = left_qn[sector]
    rows = lax.broadcasted_iota(jnp.int32, (width, width), 0)
    cols = lax.broadcasted_iota(jnp.int32, (width, width), 1)
    rows_used = rows < left_dims[sector]

    def masked(value, b):
        used = jnp.where(jnp.abs(my_qn - right_qn[b]) <= SPREAD, right_dims[b], 0)
        return jnp.where(rows_used & (cols < used), value, 0.0).astype(jnp.bfloat16)

    def left_terms(h, two):
        both = jnp.dot(
            lbuf[h].reshape(kdev * width, width), start[two], preferred_element_type=jnp.float32
        )
        both = both.astype(jnp.bfloat16).reshape(kdev, width, 2 * width)
        terms[2 * two, h] = both[:, :, :width]
        terms[2 * two + 1, h] = both[:, :, width:]

    def own_terms(two, carry):
        blocks = []
        for j in (2 * two, 2 * two + 1):
            b = right_order[j]
            blocks.append(masked(psi[b].astype(jnp.float32), b))
        start[two] = jnp.concatenate(blocks, axis=1)
        left_terms(o, two)
        return carry

    def other_terms(two, carry):
        left_terms(op, two)
        return carry

    def lanes(ref, j):
        return jnp.concatenate([ref[j, h, k] for h in range(2) for k in range(kdev)], axis=1)

    def first_value(j, b):
        value = jnp.dot(
            lanes(terms, j),
            rbuf[j].reshape(2 * kdev * width, width),
            preferred_element_type=jnp.float32,
        )
        return masked(value, b)

    def first_block(j):
        sigma[j] = first_value(j, right_order[j])

    def direct(plane, s):
        if s == 0:
            return list(range(1, nl))
        return [2 * u + (plane + s) % 2 for u in range(nl // 2)]

    def source_of(s, t):
        return ((l + nl - t) % nl) * nz + group[s]

    def first_direct(s):
        targets = [(l + t) % nl for t in direct(o, s)]
        for there in targets:
            first_block(slot_of(there, s))
        for u, there in enumerate(targets):
            send(
                sigma.at[slot_of(there, s)],
                landed.at[me],
                ssend.at[s, u],
                srecv.at[s, u],
                {"lsec": there, "rsec": group[s]},
            )

    def relay(s):
        for u in range(nl // 2):
            block = landed.at[source_of(s, direct(o, s)[u])]
            arrive(block, srecv.at[s, u])
            send(block, block, fsend.at[s, u], frecv.at[s, u], to_y)

    lax.fori_loop(0, slots // 2, own_terms, 0, unroll=2)
    stage_one(1)
    stage_two(0)
    def slot_holding(order, wanted):
        found = jnp.int32(0)
        for j in range(slots):
            found = jnp.where(order[j] == wanted, j, found)
        return found

    def find(a, carry):
        inverse_left[a] = slot_holding(left_order, a)
        return carry

    for step in range(2, nz + 3):
        if step < nz:
            stage_one(step)
        if 1 <= step - 1 < nz:
            stage_two(step - 1)
        if 0 <= step - 2 < nz:
            stage_three(step - 2)
        if step == 2:
            arrive(lbuf.at[op], lrecv)
            lax.fori_loop(0, slots // 2, other_terms, 0, unroll=2)
            lax.fori_loop(0, slots, find, 0)
        if 0 <= step - 3 < nz:
            stage_four(step - 3)
            first_direct(step - 3)
        if 0 < step - 5 < nz - 2:
            relay(step - 5)

    first_block(me)
    landed[me] = sigma[me]
    relay(nz - 2)

    count = second_ref.shape[1]
    left_wide = jnp.concatenate([lbuf[h, k] for h in range(2) for k in range(kdev)], axis=1)

    def second_pair(i, carry):
        inner = []
        for n in range(2):
            b = o * count + 2 * i + n
            j = slot_holding(right_order, b)
            state = first_value(j, b)
            part = jnp.dot(state, lanes(rbuf, j), preferred_element_type=jnp.float32)
            part = part.astype(jnp.bfloat16)
            halves = [part[:, k * width : (k + 1) * width] for k in range(2 * kdev)]
            inner.append(jnp.concatenate(halves, axis=0))
        both = jnp.dot(
            left_wide, jnp.concatenate(inner, axis=1), preferred_element_type=jnp.float32
        )
        for n in range(2):
            second[2 * i + n] = masked(
                both[:, n * width : (n + 1) * width], o * count + 2 * i + n
            )
        return carry

    relay(nz - 1)
    lax.fori_loop(0, count // 2, second_pair, 0)
    out_second = pltpu.make_async_copy(second, second_ref.at[0], osem.at[0])
    out_second.start()

    for u, t in enumerate(direct(o, 0)):
        arrive(landed.at[source_of(0, t)], srecv.at[0, u])
    for s in range(1, nz):
        for u in range(nl // 2):
            arrive(landed.at[source_of(s, direct(op, s)[u])], frecv.at[s, u])

    def place(a, carry):
        first[a] = landed[inverse_left[a]]
        return carry

    lax.fori_loop(0, slots, place, 0, unroll=4)
    out_first = pltpu.make_async_copy(first, first_ref.at[0], osem.at[1])
    out_first.start()
    for copy in sent:
        copy.wait_send()
    out_second.wait()
    out_first.wait()


def hand_over(parts, first_in, second_in, first_out, second_out, first, second, sem):
    ins, outs = [], []
    for n, (src, mid, dst) in enumerate(
        ((second_in, second, second_out), (first_in, first, first_out))
    ):
        size = mid.shape[0] // parts
        for i in range(parts):
            rows = pl.ds(i * size, size)
            ins.append(pltpu.make_async_copy(src.at[0, rows], mid.at[rows], sem.at[0, n, i]))
            outs.append(pltpu.make_async_copy(mid.at[rows], dst.at[0, rows], sem.at[1, n, i]))
    for copy in ins:
        copy.start()
    for arrived, copy in zip(ins, outs):
        arrived.wait()
        copy.start()
    for copy in outs:
        copy.wait()


def by_kernel(nz, nl, psi, left_ops, right_ops, *tables):
    slots = nl * nz
    width = psi.shape[-1]
    kdev = left_ops.shape[0]
    block = (width, width)
    dma = pltpu.SemaphoreType.DMA
    bf16 = jnp.bfloat16
    hbm = pl.BlockSpec(memory_space=pltpu.HBM)
    flops = 2 * width**3 * 2 * kdev * slots * 3
    shapes = (
        jax.ShapeDtypeStruct((1, slots) + block, bf16),
        jax.ShapeDtypeStruct((1, slots // 2) + block, bf16),
    )
    results = pl.pallas_call(
        functools.partial(kernel, nz, nl),
        out_shape=shapes,
        in_specs=[hbm] * 9,
        out_specs=(hbm, hbm),
        scratch_shapes=[
            pltpu.VMEM((slots,) + block, bf16),
            *[pltpu.SMEM(table.shape, jnp.int32) for table in tables],
            pltpu.VMEM((kdev,) + block, bf16),
            dma((9,)),
            pltpu.VMEM((slots, 2, kdev) + block, bf16),
            pltpu.VMEM((2, kdev) + block, bf16),
            pltpu.VMEM((slots // 2, width, 2 * width), bf16),
            pltpu.VMEM((slots, 2, kdev) + block, bf16),
            pltpu.VMEM((slots,) + block, bf16),
            pltpu.VMEM((slots,) + block, bf16),
            dma,
            dma,
            dma((nz,)),
            dma((nz,)),
            dma((nz,)),
            dma((nz,)),
            dma((nz,)),
            dma((nz,)),
            dma((2, nz)),
            dma((2, nz)),
            dma((2, nz)),
            dma((2, nz)),
            dma((nz, nl)),
            dma((nz, nl)),
            dma((nz, nl // 2)),
            dma((nz, nl // 2)),
            pltpu.VMEM((slots,) + block, bf16),
            pltpu.VMEM((slots // 2,) + block, bf16),
            pltpu.SMEM((slots,), jnp.int32),
            dma((2,)),
        ],
        compiler_params=pltpu.CompilerParams(
            collective_id=0, has_side_effects=True, vmem_limit_bytes=56 * 2**20
        ),
        cost_estimate=pl.CostEstimate(flops=flops, bytes_accessed=4 * 2**20, transcendentals=0),
    )(psi, left_ops, right_ops, *tables)
    parts = 4
    return pl.pallas_call(
        functools.partial(hand_over, parts),
        out_shape=shapes,
        in_specs=[hbm] * 2,
        out_specs=(hbm, hbm),
        scratch_shapes=[
            pltpu.VMEM((slots,) + block, bf16),
            pltpu.VMEM((slots // 2,) + block, bf16),
            dma((2, 2, parts)),
        ],
        compiler_params=pltpu.CompilerParams(vmem_limit_bytes=56 * 2**20),
    )(*results)


def solution(mesh):
    nl, nz, no = mesh.shape["lsec"], mesh.shape["rsec"], mesh.shape["ops"]

    def on_device(psi, left_ops, right_ops, *tables):
        gathered = no * nl * nz * left_ops.size * left_ops.dtype.itemsize
        if no == 2 and nl == 4 and nz == 4 and left_ops.shape[0] > 1 and 3 * gathered <= VMEM_BUDGET:
            return by_kernel(nz, nl, psi, left_ops, right_ops, *tables)
        return by_collectives(psi, left_ops, right_ops, *tables)

    placed = (
        P(("lsec", "rsec"), None, None, None),
        P("ops", ("lsec", "rsec"), None, None),
        P("ops", ("lsec", "rsec"), None, None),
        P(),
        P(),
        P(),
        P(),
        P(),
        P(),
    )
    return jax.shard_map(
        on_device,
        mesh=mesh,
        in_specs=placed,
        out_specs=(P(("lsec", "rsec"), None, None, None), P(("lsec", "rsec"), "ops", None, None)),
        check_vma=False,
    )
```
